32 devices in a mesh: grp: 2 (over y), tr: 4 (over z), cache: 2 (over x), sub: 2 (over core).
Axes of the slice: x: 2, y: 2, z: 4, core: 2. Of those that a mesh axis runs over, the one named last changes fastest.
Arguments:
- table: bfloat16 [32768, 768], P(('grp', 'tr', 'cache', 'sub')), parts along dimension 0, may hold values from -6 to 6
- requests: int32 [512, 64], P(('grp', 'tr', 'cache', 'sub')), parts along dimension 0, may hold values from 0 to 1023
- counts: int32 [512], P(('grp', 'tr', 'cache', 'sub')), parts along dimension 0, may hold values from 0 to 64, as said below
- nbr_low: int32 [16384, 10], P(('grp', 'tr', 'cache', 'sub')), parts along dimension 0, may hold values from 0 to 1023, as said below
- fan_low: int32 [16384], P(('grp', 'tr', 'cache', 'sub')), parts along dimension 0, may hold values from 1 to 10
- nbr_top: int32 [8192, 25], P(('grp', 'tr', 'cache', 'sub')), parts along dimension 0, may hold values from 0 to 511, as said below
- fan_top: int32 [8192], P(('grp', 'tr', 'cache', 'sub')), parts along dimension 0, may hold values from 1 to 25
- grad_logits: bfloat16 [8192, 153], P(('grp', 'tr', 'cache', 'sub')), parts along dimension 0, may hold values from -0.09375 to 0.09375
- w1_self: bfloat16 [768, 1024], replicated, may hold values from -0.21875 to 0.21875
- w1_neigh: bfloat16 [768, 1024], replicated, may hold values from -0.21875 to 0.21875
- w2_self: bfloat16 [1024, 153], replicated, may hold values from -0.1875 to 0.1875
- w2_neigh: bfloat16 [1024, 153], replicated, may hold values from -0.1875 to 0.1875
Outputs:
- logits: float32 [8192, 153], P(('grp', 'tr', 'cache', 'sub')), parts along dimension 0
- grad_w1_self: bfloat16 [1536, 1024], P('grp'), parts along dimension 0
- grad_w1_neigh: bfloat16 [1536, 1024], P('grp'), parts along dimension 0
- grad_w2_self: bfloat16 [2048, 153], P('grp'), parts along dimension 0
- grad_w2_neigh: bfloat16 [2048, 153], P('grp'), parts along dimension 0
The draws below stay inside these ranges and needn't reach their ends.
There are 2 independent parts, one for each index of `grp`. The reference program is written for one: setup_inputs(seed, part) draws one part's arguments, and reference() takes and returns one part's arrays. A program takes and returns all parts, laid end to end along the dimension named above; an argument that names none is the same for every part. Nothing has to cross between parts.
Inputs may be any that keep to these rules, and one draw needn't show every extreme that they name: `counts`: the live slots are the first ones of each trainer and owner. `nbr_low`: input node indices; entries at k >= fan_low are unused. `nbr_top`: middle node indices; entries at k >= fan_top are unused.
All inputs are finite; a program needn't handle non-finite values.
Results may differ from the reference program's by a relative error of at most 0.0059.
Values may be sent and summed in bfloat16 or wider, within the bound.
No kernel may reach another device: no remote copies, remote signals or barrier semaphores. Data moves between devices by JAX's collectives and lax.ppermute only.
A program may use at most 64 MiB of HBM per device.

```python
import jax
import jax.numpy as jnp
from jax import lax

FEAT = 768
HIDDEN_SIZE = 1024
CLASSES = 153
ROWS_DEV = 1024
SEEDS = 256
FAN_LOW = 10
FAN_TOP = 25
PEERS = 16
MIDDLE = 512
INPUTS = 1024
SLOTS = 64


def pinned_ints(key, shape, low, high):
    first_key = jax.random.fold_in(key, 0)
    pick_key = jax.random.fold_in(key, 1)
    shift_key = jax.random.fold_in(key, 3)
    values = jax.random.randint(first_key, shape, low, high, dtype=jnp.int32).reshape(-1)
    length = values.shape[0]
    first = jax.random.randint(pick_key, (), 0, length, dtype=jnp.int32)
    second = (first + 1 + jax.random.randint(shift_key, (), 0, length - 1, dtype=jnp.int32)) % length
    values = values.at[first].set(high - 1).at[second].set(low)
    return values.reshape(shape)


def draw_requests(key, part):
    key = jax.random.fold_in(key, 11)
    return pinned_ints(key, (PEERS * PEERS, SLOTS), 0, ROWS_DEV)


def draw_counts(key, part):
    key = jax.random.fold_in(key, 12)
    return pinned_ints(key, (PEERS * PEERS,), 0, SLOTS + 1)


def draw_nbr_low(key, part):
    key = jax.random.fold_in(key, 13)
    return pinned_ints(key, (PEERS * MIDDLE, FAN_LOW), 0, INPUTS)


def draw_fan_low(key, part):
    key = jax.random.fold_in(key, 14)
    return pinned_ints(key, (PEERS * MIDDLE,), 1, FAN_LOW + 1)


def draw_nbr_top(key, part):
    key = jax.random.fold_in(key, 15)
    return pinned_ints(key, (PEERS * SEEDS, FAN_TOP), 0, MIDDLE)


def draw_fan_top(key, part):
    key = jax.random.fold_in(key, 16)
    return pinned_ints(key, (PEERS * SEEDS,), 1, FAN_TOP + 1)


def block_scale(own_key, shape, cuts, least, largest):
    gain, own = 1.0, jax.random.fold_in(own_key, 6)
    for dim, parts in cuts:
        heights = jnp.exp(jax.random.uniform(jax.random.fold_in(own, dim), (parts,), jnp.float32, least / len(cuts), largest / len(cuts)))
        gain = gain * jnp.repeat(heights, shape[dim] // parts).reshape([-1 if axis == dim else 1 for axis in range(len(shape))])
    return gain


def scatter_about(rng, dims, scale, limit, shards=(), held_as=jnp.bfloat16):
    loudness = block_scale(rng, dims, shards, -0.22, 0.18) if shards else 1.0
    entries = jax.random.normal(rng, dims, jnp.float32) * scale * loudness
    return jnp.minimum(jnp.maximum(entries, -limit), limit).astype(held_as)


def setup_inputs(seed: int = 0, part: int = 0) -> dict:
    keys = jax.random.split(jax.random.key(seed), 13)
    own_keys = jax.random.split(jax.random.fold_in(keys[12], part), 13)
    table = scatter_about(own_keys[0], (PEERS * ROWS_DEV, FEAT), 1.0, 6.0, ((0, 16),))
    requests = draw_requests(jax.random.fold_in(jax.random.fold_in(keys[12], part), 71), part)
    counts = draw_counts(jax.random.fold_in(jax.random.fold_in(keys[12], part), 71), part)
    nbr_low = draw_nbr_low(jax.random.fold_in(jax.random.fold_in(keys[12], part), 71), part)
    fan_low = draw_fan_low(jax.random.fold_in(jax.random.fold_in(keys[12], part), 71), part)
    nbr_top = draw_nbr_top(jax.random.fold_in(jax.random.fold_in(keys[12], part), 71), part)
    fan_top = draw_fan_top(jax.random.fold_in(jax.random.fold_in(keys[12], part), 71), part)
    grad_logits = scatter_about(own_keys[7], (PEERS * SEEDS, CLASSES), (1.0 / (SEEDS * PEERS) ** 0.5), 0.09375, ((0, 16),))
    w1_self = scatter_about(keys[8], (FEAT, HIDDEN_SIZE), FEAT ** -0.5, 0.21875)
    w1_neigh = scatter_about(keys[9], (FEAT, HIDDEN_SIZE), FEAT ** -0.5, 0.21875)
    w2_self = scatter_about(keys[10], (HIDDEN_SIZE, CLASSES), HIDDEN_SIZE ** -0.5, 0.1875)
    w2_neigh = scatter_about(keys[11], (HIDDEN_SIZE, CLASSES), HIDDEN_SIZE ** -0.5, 0.1875)
    return {"table": table, "requests": requests, "counts": counts, "nbr_low": nbr_low, "fan_low": fan_low, "nbr_top": nbr_top, "fan_top": fan_top, "grad_logits": grad_logits, "w1_self": w1_self, "w1_neigh": w1_neigh, "w2_self": w2_self, "w2_neigh": w2_neigh}


def count_tile(neighbours, used, width):
    valid = lax.broadcasted_iota(jnp.int32, neighbours.shape, 1) < used[:, None]
    columns = lax.broadcasted_iota(jnp.int32, (neighbours.shape[0], width), 1)
    total = jnp.zeros((neighbours.shape[0], width), jnp.float32)
    for column in range(neighbours.shape[1]):
        hit = valid[:, column:column + 1] & (neighbours[:, column:column + 1] == columns)
        total = total + jnp.where(hit, 1.0, 0.0).astype(jnp.float32)
    return total.astype(jnp.bfloat16)


def train_block(inputs, nbr_low, fan_low, nbr_top, fan_top, cotangent, w1_self, w1_neigh, w2_self, w2_neigh):
    middle = nbr_low.shape[0]
    seeds = nbr_top.shape[0]
    adj_low = count_tile(nbr_low, fan_low, inputs.shape[0])
    self_low = inputs[:middle]
    div_low = fan_low[:, None].astype(jnp.float32) + 1.0
    mean_low = ((jnp.dot(adj_low, inputs, preferred_element_type=jnp.float32) + self_low.astype(jnp.float32)) / div_low).astype(jnp.bfloat16)
    pre_act = jnp.dot(self_low, w1_self, preferred_element_type=jnp.float32) + jnp.dot(mean_low, w1_neigh, preferred_element_type=jnp.float32)
    hidden = jax.nn.silu(pre_act).astype(jnp.bfloat16)
    adj_top = count_tile(nbr_top, fan_top, middle)
    self_top = hidden[:seeds]
    div_top = fan_top[:, None].astype(jnp.float32) + 1.0
    mean_top = ((jnp.dot(adj_top, hidden, preferred_element_type=jnp.float32) + self_top.astype(jnp.float32)) / div_top).astype(jnp.bfloat16)
    logits = jnp.dot(self_top, w2_self, preferred_element_type=jnp.float32) + jnp.dot(mean_top, w2_neigh, preferred_element_type=jnp.float32)
    back_top = (jnp.dot(cotangent, w2_neigh.T, preferred_element_type=jnp.float32) / div_top).astype(jnp.bfloat16)
    grad_w2s = jnp.dot(self_top.T, cotangent, preferred_element_type=jnp.float32)
    grad_w2n = jnp.dot(mean_top.T, cotangent, preferred_element_type=jnp.float32)
    direct_top = jnp.dot(cotangent, w2_self.T, preferred_element_type=jnp.float32) + back_top.astype(jnp.float32)
    grad_hidden = jnp.dot(adj_top.T, back_top, preferred_element_type=jnp.float32) + jnp.pad(direct_top, ((0, middle - seeds), (0, 0)))
    sigma = jax.nn.sigmoid(pre_act)
    grad_pre = (grad_hidden * sigma * (1.0 + pre_act * (1.0 - sigma))).astype(jnp.bfloat16)
    grad_w1s = jnp.dot(self_low.T, grad_pre, preferred_element_type=jnp.float32)
    grad_w1n = jnp.dot(mean_low.T, grad_pre, preferred_element_type=jnp.float32)
    return logits, (grad_w1s, grad_w1n, grad_w2s, grad_w2n)


def reference(table, requests, counts, nbr_low, fan_low, nbr_top, fan_top, grad_logits, w1_self, w1_neigh, w2_self, w2_neigh):
    owners = table.reshape(PEERS, ROWS_DEV, FEAT)
    owner_ids = jnp.arange(PEERS, dtype=jnp.int32)[:, None]
    slot_ids = jnp.arange(SLOTS, dtype=jnp.int32)[None, :]

    def one_trainer(carry, packed):
        asked, count_row, low_ids, low_fan, top_ids, top_fan, cotangent = packed
        fetched = owners[owner_ids, asked]
        live_slot = slot_ids < count_row[:, None]
        inputs = jnp.where(live_slot[:, :, None], fetched, jnp.zeros((), jnp.bfloat16)).reshape(INPUTS, FEAT)
        logits, grads = train_block(inputs, low_ids, low_fan, top_ids, top_fan, cotangent, w1_self, w1_neigh, w2_self, w2_neigh)
        return tuple(total + term for total, term in zip(carry, grads)), logits

    init = (jnp.zeros((FEAT, HIDDEN_SIZE), jnp.float32), jnp.zeros((FEAT, HIDDEN_SIZE), jnp.float32),
            jnp.zeros((HIDDEN_SIZE, CLASSES), jnp.float32), jnp.zeros((HIDDEN_SIZE, CLASSES), jnp.float32))
    packed = (requests.reshape(PEERS, PEERS, SLOTS), counts.reshape(PEERS, PEERS),
              nbr_low.reshape(PEERS, MIDDLE, FAN_LOW), fan_low.reshape(PEERS, MIDDLE),
              nbr_top.reshape(PEERS, SEEDS, FAN_TOP), fan_top.reshape(PEERS, SEEDS),
              grad_logits.reshape(PEERS, SEEDS, CLASSES))
    sums, logits = lax.scan(one_trainer, init, packed)
    return (logits.reshape(PEERS * SEEDS, CLASSES), sums[0].astype(jnp.bfloat16), sums[1].astype(jnp.bfloat16),
            sums[2].astype(jnp.bfloat16), sums[3].astype(jnp.bfloat16))
```

```python
import functools

import jax
import jax.numpy as jnp
from jax import lax
from jax.experimental import pallas as pl
from jax.experimental.pallas import tpu as pltpu
from jax.sharding import PartitionSpec as P

LANES = 128
BLOCKS = 8
TRAINERS = ("tr", "cache", "sub")
F32, BF16 = jnp.float32, jnp.bfloat16
VMEM = pl.BlockSpec(memory_space=pltpu.VMEM)
SMEM = pl.BlockSpec(memory_space=pltpu.SMEM)


def params(mebibytes):
    return pltpu.CompilerParams(vmem_limit_bytes=mebibytes * 1024 * 1024)


def tdot(lhs, rhs):
    return lax.dot_general(lhs, rhs, (((0,), (0,)), ((), ())), preferred_element_type=F32)


def count_tile(neighbours, used, width):
    valid = lax.broadcasted_iota(jnp.int32, neighbours.shape, 1) < used[:, None]
    columns = lax.broadcasted_iota(jnp.int32, (neighbours.shape[0], width), 1)
    total = jnp.zeros((neighbours.shape[0], width), jnp.float32)
    for column in range(neighbours.shape[1]):
        hit = valid[:, column : column + 1] & (neighbours[:, column : column + 1] == columns)
        total = total + jnp.where(hit, 1.0, 0.0).astype(jnp.float32)
    return total.astype(jnp.bfloat16)


def swap(array, axis, size, distance):
    return lax.ppermute(array, axis, [(i, i ^ distance) for i in range(size)])


def axis_bits(axis, size):
    return [(axis, size, 1 << k) for k in range(size.bit_length() - 1)]


def bit_of(step):
    axis, _, distance = step
    return lax.rem(lax.div(lax.axis_index(axis), distance), 2)


def place_of(order):
    place = jnp.int32(0)
    for step in order[:3]:
        place = 2 * place + bit_of(step)
    return place


def scatter_blocks(send, keep, order):
    for step in order[:3]:
        got = swap(send, *step)
        half = keep.shape[0] // 2
        if half:
            send = (keep[half:] + got[half:].astype(F32)).astype(BF16)
            keep = keep[:half] + got[:half].astype(F32)
        else:
            keep = keep + got.astype(F32)
    for step in order[3:]:
        half = keep.shape[1] // 2
        bit = bit_of(step)
        other = lax.dynamic_slice_in_dim(keep, (1 - bit) * half, half, 1).astype(BF16)
        keep = lax.dynamic_slice_in_dim(keep, bit * half, half, 1)
        keep = keep + swap(other, *step).astype(F32)
    return keep.astype(BF16)


def gather_blocks(share, order):
    for step in order[3:][::-1]:
        got = swap(share, *step)
        low = bit_of(step) == 0
        share = jnp.concatenate([jnp.where(low, share, got), jnp.where(low, got, share)], 1)
    for step in order[:3][::-1]:
        share = jnp.concatenate([share, swap(share, *step)], 0)
    return share


def product_kernel(rows, first, place, mine, got, grad, grad_got, *outs):
    base = 0
    for which, out in enumerate(outs):
        at = place[which]
        low = lax.rem(at, 2)
        span = slice(base, base + rows[which])
        for pair in range(BLOCKS // 4):
            column = jnp.bitwise_xor(first // 2 + pair, at // 2)
            where = pl.ds(pl.multiple_of(column * 2 * LANES, 2 * LANES), 2 * LANES)
            value = tdot(mine[:, span], grad[:, where]) + tdot(got[:, span], grad_got[:, where])
            value = value.astype(out.dtype)
            out[2 * pair + low] = value[:, :LANES]
            out[2 * pair + 1 - low] = value[:, LANES:]
        base += rows[which]


def products(rows, first, dtype, place, mine, got, grad, grad_got):
    return pl.pallas_call(
        functools.partial(product_kernel, rows, first),
        out_shape=[jax.ShapeDtypeStruct((BLOCKS // 2, r, LANES), dtype) for r in rows],
        in_specs=[SMEM, VMEM, VMEM, VMEM, VMEM],
        out_specs=[VMEM] * len(rows),
        compiler_params=params(32),
        name="grad_send" if first else "grad_keep",
    )(place, mine, got, grad, grad_got)


def place_kernel(info, *refs):
    pieces, outs = refs[:-4], refs[-4:]
    core = info[0]
    base = 0
    for which in range(len(pieces) // 2):
        own, other = pieces[2 * which], pieces[2 * which + 1]
        last = which == len(pieces) // 2 - 1
        first_out, second_out = (outs[2], outs[3]) if last else (outs[0], outs[1])
        height = first_out.shape[0] if last else own.shape[1]
        base = 0 if last else base
        span = slice(base, base + height)
        for position in range(BLOCKS):
            column = jnp.bitwise_xor(info[1 + which], position)
            where = pl.ds(pl.multiple_of(column * LANES, LANES), LANES)
            a, b = own[position, :height], other[position, :height]
            first_out[span, where] = jnp.where(core == 0, a, b)
            second_out[span, where] = jnp.where(core == 0, b, a)
        base += height


def place_blocks(info, pieces, shapes):
    return pl.pallas_call(
        place_kernel,
        out_shape=[jax.ShapeDtypeStruct(s, BF16) for s in shapes],
        in_specs=[SMEM] + [VMEM] * len(pieces),
        out_specs=[VMEM] * 4,
        compiler_params=params(32),
        name="place_blocks",
    )(info, *pieces)


def on_device(sizes, table, requests, counts, nbr_low, fan_low, nbr_top, fan_top, grad_logits,
              w1_self, w1_neigh, w2_self, w2_neigh):
    peer_count, slot_count = requests.shape
    feat_width = table.shape[1]
    middle, seeds, classes = nbr_low.shape[0], nbr_top.shape[0], grad_logits.shape[1]
    cache_bits, tr_bits = axis_bits("cache", sizes["cache"]), axis_bits("tr", sizes["tr"])
    across, along = cache_bits + tr_bits, tr_bits + cache_bits
    core = lax.axis_index("sub")
    core_step = ("sub", 2, 1)

    asked = lax.all_to_all(requests, TRAINERS, split_axis=0, concat_axis=0, tiled=True)
    picked = jnp.take(table, asked.reshape(-1), axis=0, mode="clip")
    fetched = lax.all_to_all(
        picked.reshape(peer_count, slot_count, feat_width), TRAINERS,
        split_axis=0, concat_axis=0, tiled=True,
    ).reshape(peer_count * slot_count, feat_width)

    adj_low = count_tile(nbr_low, fan_low, peer_count * slot_count)
    adj_top = count_tile(nbr_top, fan_top, middle)
    div_low = fan_low[:, None].astype(F32) + 1.0
    div_top = fan_top[:, None].astype(F32) + 1.0
    adj_low, adj_top = lax.optimization_barrier((adj_low, adj_top))
    back_top = (
        jnp.dot(grad_logits, w2_neigh.T, preferred_element_type=F32) / div_top
    ).astype(BF16)
    direct_top = jnp.dot(grad_logits, w2_self.T, preferred_element_type=F32) + back_top.astype(F32)
    grad_hidden = jnp.dot(adj_top.T, back_top, preferred_element_type=F32) + jnp.pad(
        direct_top, ((0, middle - seeds), (0, 0))
    )
    padded = -(-classes // 32) * 32
    cotangent = jnp.pad(grad_logits, ((0, 0), (0, padded - classes)))
    cotangent_got = swap(cotangent, *core_step)
    grad_hidden, cotangent, cotangent_got = lax.optimization_barrier(
        (grad_hidden, cotangent, cotangent_got)
    )

    live_slot = (
        lax.broadcasted_iota(jnp.int32, (peer_count, slot_count), 1) < counts[:, None]
    ).reshape(-1)
    inputs = jnp.where(live_slot[:, None], fetched, jnp.zeros((), BF16))
    self_low = inputs[:middle]
    mean_low = (
        (jnp.dot(adj_low, inputs, preferred_element_type=F32) + self_low.astype(F32)) / div_low
    ).astype(BF16)
    low_mine = jnp.where(core == 0, self_low, mean_low)
    low_got = swap(jnp.where(core == 0, mean_low, self_low), *core_step)
    pre_act = jnp.dot(self_low, w1_self, preferred_element_type=F32) + jnp.dot(
        mean_low, w1_neigh, preferred_element_type=F32
    )
    hidden = jax.nn.silu(pre_act).astype(BF16)
    sigma = jax.nn.sigmoid(pre_act)
    grad_pre = (grad_hidden * sigma * (1.0 + pre_act * (1.0 - sigma))).astype(BF16)
    grad_pre_got = swap(grad_pre, *core_step)

    place = jnp.stack([place_of(across), place_of(along)])
    rows = (feat_width // 2, feat_width // 2)
    sends = products(rows, BLOCKS // 2, BF16, place, low_mine, low_got, grad_pre, grad_pre_got)
    keeps = products(rows, 0, F32, place, low_mine, low_got, grad_pre, grad_pre_got)

    self_top = hidden[:seeds]
    mean_top = (
        (jnp.dot(adj_top, hidden, preferred_element_type=F32) + self_top.astype(F32)) / div_top
    ).astype(BF16)
    logits = jnp.dot(self_top, w2_self, preferred_element_type=F32) + jnp.dot(
        mean_top, w2_neigh, preferred_element_type=F32
    )
    top_mine = jnp.where(core == 0, self_top, mean_top)
    top_got = swap(jnp.where(core == 0, mean_top, self_top), *core_step)
    top_place = place[:1]
    top_send = products(
        (padded,), BLOCKS // 2, BF16, top_place, cotangent, cotangent_got, top_mine, top_got
    )
    top_keep = products((padded,), 0, F32, top_place, cotangent, cotangent_got, top_mine, top_got)

    orders = (across, along, across)
    pieces = []
    for send, keep, order in zip(list(sends) + list(top_send), list(keeps) + list(top_keep), orders):
        whole = gather_blocks(scatter_blocks(send, keep, order), order)
        pieces += [whole, swap(whole, *core_step)]
    info = jnp.concatenate([core[None].astype(jnp.int32), place, top_place])
    hidden_width = w1_self.shape[1]
    w1_shape, w2_shape = (feat_width, hidden_width), (classes, hidden_width)
    out = place_blocks(info, pieces, (w1_shape, w1_shape, w2_shape, w2_shape))
    return (logits, out[0], out[1], out[2].T, out[3].T)


def solution(mesh):
    split, whole = P(("grp", "tr", "cache", "sub"), None), P(("grp", "tr", "cache", "sub"))
    in_specs = (split, split, whole, split, whole, split, whole, split, P(), P(), P(), P())
    out_specs = (split, P("grp", None), P("grp", None), P("grp", None), P("grp", None))
    return jax.shard_map(
        functools.partial(on_device, dict(mesh.shape)),
        mesh=mesh,
        in_specs=in_specs,
        out_specs=out_specs,
        check_vma=False,
    )
```

```python
import functools

import jax
import jax.numpy as jnp
from jax import lax
from jax.experimental import pallas as pl
from jax.experimental.pallas import tpu as pltpu
from jax.sharding import PartitionSpec as P

LANES = 128
CORE_STEP = ("sub", 2, 1)
BLOCKS = 8
TRAINERS = ("tr", "cache", "sub")
F32, BF16 = jnp.float32, jnp.bfloat16
VMEM = pl.BlockSpec(memory_space=pltpu.VMEM)
SMEM = pl.BlockSpec(memory_space=pltpu.SMEM)
ANY = pl.BlockSpec(memory_space=pl.ANY)


def params(mebibytes):
    return pltpu.CompilerParams(vmem_limit_bytes=mebibytes * 1024 * 1024)


def tdot(lhs, rhs):
    return lax.dot_general(lhs, rhs, (((0,), (0,)), ((), ())), preferred_element_type=F32)


def swap(array, axis, size, distance):
    return lax.ppermute(array, axis, [(i, i ^ distance) for i in range(size)])


def axis_bits(axis, size):
    return [(axis, size, 1 << k) for k in range(size.bit_length() - 1)]


def bit_of(step):
    axis, _, distance = step
    return lax.rem(lax.div(lax.axis_index(axis), distance), 2)


def kernel_call(body, name, outs, in_specs, mebibytes, *operands, **kwargs):
    return pl.pallas_call(
        body,
        out_shape=[jax.ShapeDtypeStruct(*out) for out in outs],
        in_specs=in_specs,
        out_specs=kwargs.pop("out_specs", [VMEM] * len(outs)),
        compiler_params=params(mebibytes),
        cost_estimate=pl.CostEstimate(flops=10**10, bytes_accessed=10**7, transcendentals=0),
        name=name,
        **kwargs,
    )(*operands)


def fold_kernel(got, keep, after, send, kept):
    half = kept.shape[0]
    send[...] = (keep[half:] + got[half:].astype(F32)).astype(BF16)
    kept[...] = keep[:half] + got[:half].astype(F32)


def add_kernel(got, keep, after, out):
    out[...] = (keep[...] + got[...].astype(F32)).astype(out.dtype)


def meet_kernel(mine, got, after, out):
    out[0] = (mine[0].astype(F32) + got[1].astype(F32)).astype(BF16)
    out[1] = (mine[1].astype(F32) + got[0].astype(F32)).astype(BF16)


def join_kernel(near, far, after, out):
    half = near.shape[0]
    out[:half] = near[...]
    out[half:] = far[...]


def deep_sum(keep, order):
    extra = order[3:]
    got = swap(keep[1:].astype(BF16), *order[2])
    share = keep[:1] + got.astype(F32)
    for step in extra:
        half = share.shape[1] // 2
        bit = bit_of(step)
        other = lax.dynamic_slice_in_dim(share, (1 - bit) * half, half, 1).astype(BF16)
        share = lax.dynamic_slice_in_dim(share, bit * half, half, 1)
        share = share + swap(other, *step).astype(F32)
    share = share.astype(BF16)
    for step in extra[::-1]:
        got = swap(share, *step)
        low = bit_of(step) == 0
        share = jnp.concatenate([jnp.where(low, share, got), jnp.where(low, got, share)], 1)
    return jnp.concatenate([share, swap(share, *order[2])], 0)


class Piece:
    def __init__(self, order, got, keep):
        self.order, self.got, self.keep = order, got, keep

    def first(self, after):
        count, rows, lanes = self.keep.shape
        send, self.keep = kernel_call(
            fold_kernel, "fold", [((count // 2, rows, lanes), BF16), ((count // 2, rows, lanes), F32)],
            [VMEM, VMEM, ANY], 16, self.got, self.keep, after,
        )
        self.got = swap(send, *self.order[1])
        return send

    def second(self, after):
        deep = len(self.order) > 3
        self.keep, = kernel_call(
            add_kernel, "add", [(self.keep.shape, F32 if deep else BF16)],
            [VMEM, VMEM, ANY], 16, self.got, self.keep, after,
        )
        if not deep:
            self.got = swap(self.keep, *self.order[2])
        return self.keep

    def meet(self, after):
        if len(self.order) > 3:
            self.keep = deep_sum(self.keep, self.order)
        else:
            self.keep, = kernel_call(
                meet_kernel, "meet", [(self.keep.shape, BF16)],
                [VMEM, VMEM, ANY], 16, self.keep, self.got, after,
            )
        self.got = swap(self.keep, *self.order[1])
        return self.keep

    def join(self, after):
        count, rows, lanes = self.keep.shape
        near, = kernel_call(
            join_kernel, "join", [((2 * count, rows, lanes), BF16)],
            [VMEM, VMEM, ANY], 16, self.keep, self.got, after,
        )
        far = swap(near, *self.order[0])
        self.blocks = (near, far, swap(near, *CORE_STEP))
        return near


def pair_of(info):
    return lax.rem(lax.div(info[1], 2), 2), lax.rem(info[1], 2)


def gradient(span, columns, mine, got, grad, grad_got):
    return tdot(mine[:, span], grad[:, columns]) + tdot(got[:, span], grad_got[:, columns])


def wide_pair(pair):
    return pl.ds(pl.multiple_of(pair * 2 * LANES, 2 * LANES), 2 * LANES)


def across_blocks(info, span, rows, mine, got, grad, grad_got, out):
    high, low = pair_of(info)
    for pair in range(2):
        value = gradient(span, wide_pair(jnp.bitwise_xor(pair, high)), mine, got, grad, grad_got)
        value = value.astype(out.dtype)
        out[2 * pair + low, rows] = value[:, :LANES]
        out[2 * pair + 1 - low, rows] = value[:, LANES:]


def along_blocks(info, first, span, mine, got, halves, out):
    high, low = pair_of(info)
    for bit, (grad, grad_got) in enumerate(halves):
        value = gradient(span, wide_pair(jnp.bitwise_xor(first, high)), mine, got, grad, grad_got)
        value = value.astype(out.dtype)
        out[2 * low + bit] = value[:, :LANES]
        out[2 * (1 - low) + bit] = value[:, LANES:]


def send_across_kernel(base, info, mine, got, grad, grad_got, after, out):
    rows = out.shape[1]
    across_blocks(info, slice(base, base + rows), slice(0, rows), mine, got, grad, grad_got, out)


def send_along_kernel(base, info, mine, got, grad, grad_got, far, far_got, after, out):
    span = slice(base, base + out.shape[1])
    along_blocks(info, 1, span, mine, got, ((grad, grad_got), (far, far_got)), out)


def keep_kernel(info, mine, got, grad, grad_got, far, far_got, after, out, out_along):
    rows = out.shape[1]
    across_blocks(info, slice(0, rows), slice(0, rows), mine, got, grad, grad_got, out)
    span = slice(rows, 2 * rows)
    along_blocks(info, 0, span, mine, got, ((grad, grad_got), (far, far_got)), out_along)


def last_kernel(base, info, mine, got, grad, grad_got, far, far_got, cot, cot_got, top, top_got,
                top_far, top_far_got, after, send, keep):
    rows, more = mine.shape[1] - base, cot.shape[1]
    for out, a, b, c, d in (
        (send, far, far_got, top_far, top_far_got), (keep, grad, grad_got, top, top_got)
    ):
        across_blocks(info, slice(base, base + rows), slice(0, rows), mine, got, a, b, out)
        across_blocks(info, slice(0, more), slice(rows, rows + more), cot, cot_got, c, d, out)


def pick_kernel(asked, table, out, done, onehot, held, sem):
    copy = pltpu.make_async_copy(table, held, sem)
    copy.start()
    peers, slots = asked.shape
    wide = lax.broadcasted_iota(jnp.int32, (16 * max(1, slots // 16), table.shape[0]), 1)
    columns = asked[...].T
    step = max(1, 16 // slots)
    for peer in range(0, peers, step):
        numbers = [columns[:, p : p + 1] for p in range(peer, peer + step)]
        numbers = numbers[0] if step == 1 else jnp.concatenate(numbers, 0)
        onehot[peer * slots : (peer + step) * slots] = jnp.where(numbers == wide, 1.0, 0.0).astype(BF16)
    done[...] = jnp.zeros_like(done)
    copy.wait()
    for start in range(0, out.shape[1], 256):
        span = slice(start, start + 256)
        out[:, span] = jnp.dot(onehot[...], held[:, span], preferred_element_type=F32).astype(BF16)


def pick_rows(asked, table):
    total = asked.shape[0] * asked.shape[1]
    return pl.pallas_call(
        pick_kernel,
        out_shape=[
            jax.ShapeDtypeStruct((total, table.shape[1]), BF16),
            jax.ShapeDtypeStruct((8, LANES), jnp.int32),
        ],
        in_specs=[VMEM, ANY],
        out_specs=[VMEM, VMEM],
        scratch_shapes=[
            pltpu.VMEM((total, table.shape[0]), BF16),
            pltpu.VMEM(table.shape, BF16),
            pltpu.SemaphoreType.DMA,
        ],
        compiler_params=params(56),
        name="pick_rows",
    )(asked, table)


def column_of(row):
    return jnp.broadcast_to(row, (8, row.shape[1])).T[:, :1]


def count_kernel(neighbours, used, held, adjacency, live, tile):
    slots, count = neighbours.shape
    held[...] = jnp.full(held.shape, -1, jnp.int32)
    slot = lax.broadcasted_iota(jnp.int32, (slots, count), 0)
    held[:slots] = jnp.where(slot < used[...], neighbours[...], -1)
    columns = held[...].T
    wide = lax.broadcasted_iota(jnp.int32, (tile, adjacency.shape[1]), 1)
    for start in range(0, count, tile):
        total = jnp.zeros(wide.shape, F32)
        for k in range(slots):
            total = total + jnp.where(columns[start : start + tile, k : k + 1] == wide, 1.0, 0.0)
        if live is not None:
            total = total * live
        adjacency[start : start + tile] = total.astype(BF16)


def beside_kernel(counts, nbr_low, fan_low, nbr_top, fan_top, grad, w2_self, w2_neigh, done,
                  adj_low, adj_top, sides, scale_top, grad_hidden, cotangent,
                  held_low, held_top, held_grad):
    peers = counts.shape[0]
    slots = adj_low.shape[1] // peers
    lane = lax.broadcasted_iota(jnp.int32, (1, adj_low.shape[1]), 1)
    live = jnp.zeros(lane.shape, F32)
    for peer in range(peers):
        here = (lane >= peer * slots) & (lane < peer * slots + counts[peer])
        live = jnp.where(here, 1.0, live)
    count_kernel(nbr_low, fan_low, held_low, adj_low, live, 32)
    count_kernel(nbr_top, fan_top, held_top, adj_top, None, 64)
    sides[:, :1] = column_of(1.0 / (fan_low[...].astype(F32) + 1.0))
    sides[:, 1:] = column_of(live[:, : sides.shape[0]])
    scale = column_of(1.0 / (fan_top[...].astype(F32) + 1.0))
    scale_top[...] = scale
    held_grad[...] = jnp.zeros_like(held_grad)
    held_grad[: grad.shape[0]] = grad[...].astype(F32)
    cotangent[...] = held_grad[...].T.astype(BF16)
    back = (tdot(grad[...], w2_neigh[...]) * scale).astype(BF16)
    direct = tdot(grad[...], w2_self[...]) + back.astype(F32)
    seeds = back.shape[0]
    for start in range(0, grad_hidden.shape[1], 256):
        span = slice(start, start + 256)
        spread = tdot(adj_top[...], back[:, span])
        grad_hidden[:seeds, span] = (spread[:seeds] + direct[:, span]).astype(grad_hidden.dtype)
        grad_hidden[seeds:, span] = spread[seeds:].astype(grad_hidden.dtype)


def beside(inputs, padded, counts, nbr_low, fan_low, nbr_top, fan_top, grad, w2_self, w2_neigh, done):
    middle, seeds, hidden = nbr_low.shape[1], nbr_top.shape[1], w2_self.shape[1]
    shape = jax.ShapeDtypeStruct
    return pl.pallas_call(
        beside_kernel,
        out_shape=[
            shape((middle, inputs), BF16), shape((seeds, middle), BF16), shape((middle, 2), F32),
            shape((seeds, 1), F32), shape((middle, hidden), BF16), shape((seeds, padded), BF16),
        ],
        in_specs=[SMEM] + [VMEM] * 7 + [ANY],
        out_specs=[VMEM] * 6,
        scratch_shapes=[
            pltpu.VMEM((-(-nbr_low.shape[0] // 8) * 8, middle), jnp.int32),
            pltpu.VMEM((-(-nbr_top.shape[0] // 8) * 8, seeds), jnp.int32),
            pltpu.VMEM((padded, seeds), F32),
        ],
        compiler_params=params(32),
        cost_estimate=pl.CostEstimate(flops=10**10, bytes_accessed=10**7, transcendentals=0),
        name="beside",
    )(counts, nbr_low, fan_low, nbr_top, fan_top, grad, w2_self, w2_neigh, done)


def mean_kernel(info, fetched, sides, adjacency, mine, other):
    first = info[0] == 0
    middle = mine.shape[0]
    for start in range(0, mine.shape[1], 256):
        span = slice(start, start + 256)
        own = jnp.where(sides[:, 1:] > 0.0, fetched[:middle, span].astype(F32), 0.0)
        total = jnp.dot(adjacency[...], fetched[:, span], preferred_element_type=F32)
        mean = (total + own) * sides[:, :1]
        mine[:, span] = jnp.where(first, own, mean).astype(BF16)
        other[:, span] = jnp.where(first, mean, own).astype(BF16)


def hidden_kernel(which, info, mine, other, w1_self, w1_neigh, grad_hidden, after, hidden, grad_pre):
    first = info[0] == 0
    width = hidden.shape[1]
    base = jnp.bitwise_xor(lax.div(info[1], 4), which) * width
    own = jnp.where(first, mine[...], other[...])
    mean = jnp.where(first, other[...], mine[...])
    for start in range(0, width, 256):
        at = pl.ds(pl.multiple_of(base + start, 256), 256)
        span = slice(start, start + 256)
        pre_act = jnp.dot(own, w1_self[:, at], preferred_element_type=F32)
        pre_act = pre_act + jnp.dot(mean, w1_neigh[:, at], preferred_element_type=F32)
        sigma = jax.nn.sigmoid(pre_act)
        hidden[:, span] = (pre_act * sigma).astype(BF16)
        grad = grad_hidden[:, at].astype(F32) * sigma * (1.0 + pre_act * (1.0 - sigma))
        grad_pre[:, span] = grad.astype(BF16)


def top_kernel(info, near, far, adjacency, scale, w2_self, w2_neigh, after,
               logits, mine_near, mine_far, other_near, other_far):
    first = info[0] == 0
    seeds, width = mine_near.shape
    dims = (((1,), (1,)), ((), ()))
    total = jnp.zeros(logits.shape, F32)
    for which, (hidden, mine, other) in enumerate(((near, mine_near, other_near), (far, mine_far, other_far))):
        at = pl.multiple_of(jnp.bitwise_xor(lax.div(info[1], 4), which) * width, width)
        own = hidden[:seeds]
        mean = jnp.dot(adjacency[...], hidden[...], preferred_element_type=F32)
        mean = ((mean + own.astype(F32)) * scale[...]).astype(BF16)
        mine[...] = jnp.where(first, own, mean)
        other[...] = jnp.where(first, mean, own)
        columns = pl.ds(at, width)
        total = total + lax.dot_general(w2_self[:, columns], own, dims, preferred_element_type=F32)
        total = total + lax.dot_general(w2_neigh[:, columns], mean, dims, preferred_element_type=F32)
    logits[...] = total


def column_at(info, along, position):
    bits = (position % 2) * 4 + position // 2 if along else position
    return pl.ds(pl.multiple_of(jnp.bitwise_xor(info[1], bits) * LANES, LANES), LANES)


def place_kernel(bases, info, *refs):
    pieces, outs, tops, held, sems = refs[:12], refs[12:14], refs[14:16], refs[16], refs[17]
    core, feat, more = info[0], held.shape[1], tops[0].shape[0]
    copies = []
    for which, base in enumerate(bases):
        near, far, near_other, far_other = pieces[4 * which : 4 * which + 4]
        last = which == len(bases) - 1
        rows = (feat if last else bases[which + 1]) - base
        span = slice(base, base + rows)
        for position in range(BLOCKS):
            where = column_at(info, which == 1, position)
            index = position % (BLOCKS // 2)
            own, other = (near, near_other) if position < BLOCKS // 2 else (far, far_other)
            a, b = own[index], other[index]
            for kind in range(2):
                value = jnp.where(core == kind, a, b)
                held[kind, span, where] = value[:rows]
                if last:
                    tops[kind][:, where] = value[rows : rows + more]
        for kind in range(2):
            copies.append(
                pltpu.make_async_copy(
                    held.at[kind, span], outs[kind].at[pl.ds(base, rows)], sems.at[which, kind]
                )
            )
            copies[-1].start()
    for copy in copies:
        copy.wait()


def place_blocks(info, bases, feat, more, width, pieces):
    shapes = [((feat, width), BF16)] * 2 + [((more, width), BF16)] * 2
    return kernel_call(
        functools.partial(place_kernel, bases), "place", shapes, [SMEM] + [VMEM] * 12, 24, info, *pieces,
        out_specs=[ANY, ANY, VMEM, VMEM],
        scratch_shapes=[pltpu.VMEM((2, feat, width), BF16), pltpu.SemaphoreType.DMA((len(bases), 2))],
    )


def on_device(sizes, table, requests, counts, nbr_low, fan_low, nbr_top, fan_top, grad_logits,
              w1_self, w1_neigh, w2_self, w2_neigh):
    peer_count, slot_count = requests.shape
    feat, width = w1_self.shape
    middle, seeds, classes = nbr_low.shape[0], nbr_top.shape[0], grad_logits.shape[1]
    across = axis_bits("cache", sizes["cache"]) + axis_bits("tr", sizes["tr"])
    along = across[1:3] + across[:1] + across[3:]
    place = 4 * bit_of(across[0]) + 2 * bit_of(across[1]) + bit_of(across[2])
    info = jnp.stack([lax.axis_index("sub"), place]).astype(jnp.int32)
    padded = -(-classes // 32) * 32
    part = (feat + padded) // 48 * 16
    last = feat - 2 * part

    asked = lax.all_to_all(requests, TRAINERS, split_axis=0, concat_axis=0, tiled=True)
    picked, done = pick_rows(asked, table)
    fetched = lax.all_to_all(
        picked.reshape(peer_count, slot_count, feat), TRAINERS, split_axis=0, concat_axis=0, tiled=True
    ).reshape(peer_count * slot_count, feat)

    adj_low, adj_top, sides, scale_top, grad_hidden, cotangent = beside(
        peer_count * slot_count, padded, counts, nbr_low.T, fan_low[None], nbr_top.T, fan_top[None],
        grad_logits.T, w2_self.T, w2_neigh.T, done,
    )
    cotangent_got = swap(cotangent, *CORE_STEP)

    low = ((middle, feat), BF16)
    mine, other = kernel_call(
        mean_kernel, "mean", [low, low], [SMEM] + [VMEM] * 3, 24, info, fetched, sides, adj_low,
    )
    got = swap(other, *CORE_STEP)
    half = ((middle, width // 2), BF16)
    hidden, grads, grads_got = [None] * 2, [None] * 2, [None] * 2
    after = mine
    for which in (1, 0):
        hidden[which], grads[which] = kernel_call(
            functools.partial(hidden_kernel, which), "hidden", [half, half], [SMEM] + [VMEM] * 5 + [ANY], 24,
            info, mine, other, w1_self, w1_neigh, grad_hidden, after,
        )
        grads_got[which] = swap(grads[which], *CORE_STEP)
        after = grads[which]
    send_half, keep_half = (grads[1], grads_got[1]), (grads[0], grads_got[0])

    blocks = (BLOCKS // 2, part, LANES)
    first_send, = kernel_call(
        functools.partial(send_across_kernel, 0), "send_across", [(blocks, BF16)],
        [SMEM] + [VMEM] * 4 + [ANY], 24, info, mine, got, *send_half, after,
    )
    first_got = swap(first_send, *across[0])
    second_send, = kernel_call(
        functools.partial(send_along_kernel, part), "send_along", [(blocks, BF16)],
        [SMEM] + [VMEM] * 6 + [ANY], 24, info, mine, got, *keep_half, *send_half, first_send,
    )
    second_got = swap(second_send, *along[0])
    top = ((seeds, width // 2), BF16)
    logits, *tops = kernel_call(
        top_kernel, "top", [((classes, seeds), F32), top, top, top, top], [SMEM] + [VMEM] * 6 + [ANY], 24,
        info, hidden[0], hidden[1], adj_top, scale_top, w2_self.T, w2_neigh.T, second_send,
    )
    tops_got = [swap(tops[2], *CORE_STEP), swap(tops[3], *CORE_STEP)]
    first_keep, second_keep = kernel_call(
        keep_kernel, "keep", [(blocks, F32), (blocks, F32)], [SMEM] + [VMEM] * 6 + [ANY], 24,
        info, mine, got, *keep_half, *send_half, logits,
    )
    blocks = (BLOCKS // 2, last + padded, LANES)
    third_send, third_keep = kernel_call(
        functools.partial(last_kernel, 2 * part), "last", [(blocks, BF16), (blocks, F32)],
        [SMEM] + [VMEM] * 12 + [ANY], 24, info, mine, got, *keep_half, *send_half, cotangent, cotangent_got,
        tops[0], tops_got[0], tops[1], tops_got[1], second_keep,
    )
    third_got = swap(third_send, *across[0])
    a = Piece(across, first_got, first_keep)
    b = Piece(along, second_got, second_keep)
    c = Piece(across, third_got, third_keep)
    after = third_keep
    for step in (a.first, b.first, a.second, c.first, b.second, c.second,
                 a.meet, b.meet, a.join, c.meet, b.join, c.join):
        after = step(after)

    def both_kinds(piece):
        near, far, near_other = piece.blocks
        return near, far, near_other, swap(far, *CORE_STEP)

    pieces = both_kinds(a) + both_kinds(b) + both_kinds(c)
    w1s, w1n, w2s, w2n = place_blocks(info, (0, part, 2 * part), feat, classes, width, pieces)
    return (logits.T, w1s, w1n, w2s.T, w2n.T)


def solution(mesh):
    split, whole = P(("grp", "tr", "cache", "sub"), None), P(("grp", "tr", "cache", "sub"))
    in_specs = (split, split, whole, split, whole, split, whole, split, P(), P(), P(), P())
    out_specs = (split, P("grp", None), P("grp", None), P("grp", None), P("grp", None))
    return jax.shard_map(
        functools.partial(on_device, dict(mesh.shape)),
        mesh=mesh,
        in_specs=in_specs,
        out_specs=out_specs,
        check_vma=False,
    )
```

```python
import functools

import jax
import jax.numpy as jnp
from jax import lax
from jax.experimental import pallas as pl
from jax.experimental.pallas import tpu as pltpu
from jax.sharding import PartitionSpec as P

LANES = 128
CORE_STEP = ("sub", 2, 1)
BLOCKS = 8
TRAINERS = ("tr", "cache", "sub")
F32, BF16 = jnp.float32, jnp.bfloat16
VMEM = pl.BlockSpec(memory_space=pltpu.VMEM)
SMEM = pl.BlockSpec(memory_space=pltpu.SMEM)
ANY = pl.BlockSpec(memory_space=pl.ANY)


def params(mebibytes):
    return pltpu.CompilerParams(vmem_limit_bytes=mebibytes * 1024 * 1024)


def tdot(lhs, rhs):
    return lax.dot_general(lhs, rhs, (((0,), (0,)), ((), ())), preferred_element_type=F32)


def swap(array, axis, size, distance):
    return lax.ppermute(array, axis, [(i, i ^ distance) for i in range(size)])


def axis_bits(axis, size):
    return [(axis, size, 1 << k) for k in range(size.bit_length() - 1)]


def bit_of(step):
    axis, _, distance = step
    return lax.rem(lax.div(lax.axis_index(axis), distance), 2)


def kernel_call(body, name, outs, in_specs, mebibytes, *operands, **kwargs):
    return pl.pallas_call(
        body,
        out_shape=[jax.ShapeDtypeStruct(*out) for out in outs],
        in_specs=in_specs,
        out_specs=kwargs.pop("out_specs", [VMEM] * len(outs)),
        compiler_params=params(mebibytes),
        cost_estimate=pl.CostEstimate(flops=10**10, bytes_accessed=10**7, transcendentals=0),
        name=name,
        **kwargs,
    )(*operands)


def fold_kernel(got, keep, after, send, kept):
    half = kept.shape[0]
    send[...] = (keep[half:] + got[half:].astype(F32)).astype(BF16)
    kept[...] = keep[:half] + got[:half].astype(F32)


def add_kernel(got, keep, after, out):
    out[...] = (keep[...] + got[...].astype(F32)).astype(out.dtype)


def meet_kernel(mine, got, after, out):
    out[0] = (mine[0].astype(F32) + got[1].astype(F32)).astype(BF16)
    out[1] = (mine[1].astype(F32) + got[0].astype(F32)).astype(BF16)


def join_kernel(near, far, after, later, out):
    half = near.shape[0]
    out[:half] = near[...]
    out[half:] = far[...]


def deep_sum(keep, order):
    extra = order[3:]
    got = swap(keep[1:].astype(BF16), *order[2])
    share = keep[:1] + got.astype(F32)
    for step in extra:
        half = share.shape[1] // 2
        bit = bit_of(step)
        other = lax.dynamic_slice_in_dim(share, (1 - bit) * half, half, 1).astype(BF16)
        share = lax.dynamic_slice_in_dim(share, bit * half, half, 1)
        share = share + swap(other, *step).astype(F32)
    share = share.astype(BF16)
    for step in extra[::-1]:
        got = swap(share, *step)
        low = bit_of(step) == 0
        share = jnp.concatenate([jnp.where(low, share, got), jnp.where(low, got, share)], 1)
    return jnp.concatenate([share, swap(share, *order[2])], 0)


class Piece:
    def __init__(self, order, got, keep):
        self.order, self.got, self.keep = order, got, keep

    def first(self, after):
        count, rows, lanes = self.keep.shape
        send, self.keep = kernel_call(
            fold_kernel, "fold", [((count // 2, rows, lanes), BF16), ((count // 2, rows, lanes), F32)],
            [VMEM, VMEM, ANY], 16, self.got, self.keep, after,
        )
        self.got = swap(send, *self.order[1])
        return send

    def second(self, after):
        deep = len(self.order) > 3
        self.keep, = kernel_call(
            add_kernel, "add", [(self.keep.shape, F32 if deep else BF16)],
            [VMEM, VMEM, ANY], 16, self.got, self.keep, after,
        )
        if not deep:
            self.got = swap(self.keep, *self.order[2])
        return self.keep

    def meet(self, after):
        if len(self.order) > 3:
            self.keep = deep_sum(self.keep, self.order)
        else:
            self.keep, = kernel_call(
                meet_kernel, "meet", [(self.keep.shape, BF16)],
                [VMEM, VMEM, ANY], 16, self.keep, self.got, after,
            )
        self.got = swap(self.keep, *self.order[1])
        return self.keep

    def join(self, after, later):
        count, rows, lanes = self.keep.shape
        near, = kernel_call(
            join_kernel, "join", [((2 * count, rows, lanes), BF16)],
            [VMEM, VMEM, ANY, ANY], 16, self.keep, self.got, after, later,
        )
        far = swap(near, *self.order[0])
        self.blocks = (near, far, swap(near, *CORE_STEP))
        return near


def pair_of(info):
    return lax.rem(lax.div(info[1], 2), 2), lax.rem(info[1], 2)


def gradient(span, columns, mine, got, grad, grad_got):
    return tdot(mine[:, span], grad[:, columns]) + tdot(got[:, span], grad_got[:, columns])


def wide_pair(pair):
    return pl.ds(pl.multiple_of(pair * 2 * LANES, 2 * LANES), 2 * LANES)


def across_blocks(info, span, rows, mine, got, grad, grad_got, out):
    high, low = pair_of(info)
    for pair in range(2):
        value = gradient(span, wide_pair(jnp.bitwise_xor(pair, high)), mine, got, grad, grad_got)
        value = value.astype(out.dtype)
        out[2 * pair + low, rows] = value[:, :LANES]
        out[2 * pair + 1 - low, rows] = value[:, LANES:]


def along_blocks(info, first, span, mine, got, halves, out):
    high, low = pair_of(info)
    for bit, (grad, grad_got) in enumerate(halves):
        value = gradient(span, wide_pair(jnp.bitwise_xor(first, high)), mine, got, grad, grad_got)
        value = value.astype(out.dtype)
        out[2 * low + bit] = value[:, :LANES]
        out[2 * (1 - low) + bit] = value[:, LANES:]


def send_across_kernel(base, info, mine, got, grad, grad_got, after, out):
    rows = out.shape[1]
    across_blocks(info, slice(base, base + rows), slice(0, rows), mine, got, grad, grad_got, out)


def send_along_kernel(base, info, mine, got, grad, grad_got, far, far_got, after, out):
    span = slice(base, base + out.shape[1])
    along_blocks(info, 1, span, mine, got, ((grad, grad_got), (far, far_got)), out)


def keep_kernel(info, mine, got, grad, grad_got, far, far_got, after, out, out_along):
    rows = out.shape[1]
    across_blocks(info, slice(0, rows), slice(0, rows), mine, got, grad, grad_got, out)
    span = slice(rows, 2 * rows)
    along_blocks(info, 0, span, mine, got, ((grad, grad_got), (far, far_got)), out_along)


def last_kernel(base, info, mine, got, grad, grad_got, far, far_got, cot, cot_got, top, top_got,
                top_far, top_far_got, after, send, keep):
    rows, more = mine.shape[1] - base, cot.shape[1]
    for out, a, b, c, d in (
        (send, far, far_got, top_far, top_far_got), (keep, grad, grad_got, top, top_got)
    ):
        across_blocks(info, slice(base, base + rows), slice(0, rows), mine, got, a, b, out)
        across_blocks(info, slice(0, more), slice(rows, rows + more), cot, cot_got, c, d, out)


def pick_kernel(asked, table, out, done, onehot, held, sem):
    copy = pltpu.make_async_copy(table, held, sem)
    copy.start()
    peers, slots = asked.shape
    wide = lax.broadcasted_iota(jnp.int32, (16 * max(1, slots // 16), table.shape[0]), 1)
    columns = asked[...].T
    step = max(1, 16 // slots)
    for peer in range(0, peers, step):
        numbers = [columns[:, p : p + 1] for p in range(peer, peer + step)]
        numbers = numbers[0] if step == 1 else jnp.concatenate(numbers, 0)
        onehot[peer * slots : (peer + step) * slots] = jnp.where(numbers == wide, 1.0, 0.0).astype(BF16)
    done[...] = jnp.zeros_like(done)
    copy.wait()
    for start in range(0, out.shape[1], 256):
        span = slice(start, start + 256)
        out[:, span] = jnp.dot(onehot[...], held[:, span], preferred_element_type=F32).astype(BF16)


def pick_rows(asked, table):
    total = asked.shape[0] * asked.shape[1]
    return pl.pallas_call(
        pick_kernel,
        out_shape=[
            jax.ShapeDtypeStruct((total, table.shape[1]), BF16),
            jax.ShapeDtypeStruct((8, LANES), jnp.int32),
        ],
        in_specs=[VMEM, ANY],
        out_specs=[VMEM, VMEM],
        scratch_shapes=[
            pltpu.VMEM((total, table.shape[0]), BF16),
            pltpu.VMEM(table.shape, BF16),
            pltpu.SemaphoreType.DMA,
        ],
        compiler_params=params(56),
        name="pick_rows",
    )(asked, table)


def column_of(row):
    return jnp.broadcast_to(row, (8, row.shape[1])).T[:, :1]


def count_kernel(neighbours, used, held, adjacency, live, tile):
    slots, count = neighbours.shape
    held[...] = jnp.full(held.shape, -1, jnp.int32)
    slot = lax.broadcasted_iota(jnp.int32, (slots, count), 0)
    held[:slots] = jnp.where(slot < used[...], neighbours[...], -1)
    columns = held[...].T
    wide = lax.broadcasted_iota(jnp.int32, (tile, adjacency.shape[1]), 1)
    for start in range(0, count, tile):
        total = jnp.zeros(wide.shape, F32)
        for k in range(slots):
            total = total + jnp.where(columns[start : start + tile, k : k + 1] == wide, 1.0, 0.0)
        if live is not None:
            total = total * live
        adjacency[start : start + tile] = total.astype(BF16)


def beside_kernel(counts, nbr_low, fan_low, nbr_top, fan_top, grad, w2_self, w2_neigh, done,
                  adj_low, adj_top, sides, scale_top, grad_hidden, cotangent,
                  held_low, held_top, held_grad):
    peers = counts.shape[0]
    slots = adj_low.shape[1] // peers
    lane = lax.broadcasted_iota(jnp.int32, (1, adj_low.shape[1]), 1)
    live = jnp.zeros(lane.shape, F32)
    for peer in range(peers):
        here = (lane >= peer * slots) & (lane < peer * slots + counts[peer])
        live = jnp.where(here, 1.0, live)
    count_kernel(nbr_low, fan_low, held_low, adj_low, live, 32)
    count_kernel(nbr_top, fan_top, held_top, adj_top, None, 64)
    sides[:, :1] = column_of(1.0 / (fan_low[...].astype(F32) + 1.0))
    sides[:, 1:] = column_of(live[:, : sides.shape[0]])
    scale = column_of(1.0 / (fan_top[...].astype(F32) + 1.0))
    scale_top[...] = scale
    held_grad[...] = jnp.zeros_like(held_grad)
    held_grad[: grad.shape[0]] = grad[...].astype(F32)
    cotangent[...] = held_grad[...].T.astype(BF16)
    back = (tdot(grad[...], w2_neigh[...]) * scale).astype(BF16)
    direct = tdot(grad[...], w2_self[...]) + back.astype(F32)
    seeds = back.shape[0]
    for start in range(0, grad_hidden.shape[1], 256):
        span = slice(start, start + 256)
        spread = tdot(adj_top[...], back[:, span])
        grad_hidden[:seeds, span] = (spread[:seeds] + direct[:, span]).astype(grad_hidden.dtype)
        grad_hidden[seeds:, span] = spread[seeds:].astype(grad_hidden.dtype)


def beside(inputs, padded, counts, nbr_low, fan_low, nbr_top, fan_top, grad, w2_self, w2_neigh, done):
    middle, seeds, hidden = nbr_low.shape[1], nbr_top.shape[1], w2_self.shape[1]
    shape = jax.ShapeDtypeStruct
    return pl.pallas_call(
        beside_kernel,
        out_shape=[
            shape((middle, inputs), BF16), shape((seeds, middle), BF16), shape((middle, 2), F32),
            shape((seeds, 1), F32), shape((middle, hidden), BF16), shape((seeds, padded), BF16),
        ],
        in_specs=[SMEM] + [VMEM] * 7 + [ANY],
        out_specs=[VMEM] * 6,
        scratch_shapes=[
            pltpu.VMEM((-(-nbr_low.shape[0] // 8) * 8, middle), jnp.int32),
            pltpu.VMEM((-(-nbr_top.shape[0] // 8) * 8, seeds), jnp.int32),
            pltpu.VMEM((padded, seeds), F32),
        ],
        compiler_params=params(32),
        cost_estimate=pl.CostEstimate(flops=10**10, bytes_accessed=10**7, transcendentals=0),
        name="beside",
    )(counts, nbr_low, fan_low, nbr_top, fan_top, grad, w2_self, w2_neigh, done)


def mean_kernel(info, fetched, sides, adjacency, mine, other):
    first = info[0] == 0
    middle = mine.shape[0]
    for start in range(0, mine.shape[1], 256):
        span = slice(start, start + 256)
        own = jnp.where(sides[:, 1:] > 0.0, fetched[:middle, span].astype(F32), 0.0)
        total = jnp.dot(adjacency[...], fetched[:, span], preferred_element_type=F32)
        mean = (total + own) * sides[:, :1]
        mine[:, span] = jnp.where(first, own, mean).astype(BF16)
        other[:, span] = jnp.where(first, mean, own).astype(BF16)


def hidden_kernel(which, info, mine, other, w1_self, w1_neigh, grad_hidden, after, hidden, grad_pre):
    first = info[0] == 0
    width = hidden.shape[1]
    base = jnp.bitwise_xor(lax.div(info[1], 4), which) * width
    own = jnp.where(first, mine[...], other[...])
    mean = jnp.where(first, other[...], mine[...])
    for start in range(0, width, 256):
        at = pl.ds(pl.multiple_of(base + start, 256), 256)
        span = slice(start, start + 256)
        pre_act = jnp.dot(own, w1_self[:, at], preferred_element_type=F32)
        pre_act = pre_act + jnp.dot(mean, w1_neigh[:, at], preferred_element_type=F32)
        sigma = jax.nn.sigmoid(pre_act)
        hidden[:, span] = (pre_act * sigma).astype(BF16)
        grad = grad_hidden[:, at].astype(F32) * sigma * (1.0 + pre_act * (1.0 - sigma))
        grad_pre[:, span] = grad.astype(BF16)


def top_kernel(info, near, far, adjacency, scale, w2_self, w2_neigh, after,
               logits, mine_near, mine_far, other_near, other_far):
    first = info[0] == 0
    seeds, width = mine_near.shape
    dims = (((1,), (1,)), ((), ()))
    total = jnp.zeros(logits.shape, F32)
    for which, (hidden, mine, other) in enumerate(((near, mine_near, other_near), (far, mine_far, other_far))):
        at = pl.multiple_of(jnp.bitwise_xor(lax.div(info[1], 4), which) * width, width)
        own = hidden[:seeds]
        mean = jnp.dot(adjacency[...], hidden[...], preferred_element_type=F32)
        mean = ((mean + own.astype(F32)) * scale[...]).astype(BF16)
        mine[...] = jnp.where(first, own, mean)
        other[...] = jnp.where(first, mean, own)
        columns = pl.ds(at, width)
        total = total + lax.dot_general(w2_self[:, columns], own, dims, preferred_element_type=F32)
        total = total + lax.dot_general(w2_neigh[:, columns], mean, dims, preferred_element_type=F32)
    logits[...] = total


def column_at(info, along, position):
    bits = (position % 2) * 4 + position // 2 if along else position
    return pl.ds(pl.multiple_of(jnp.bitwise_xor(info[1], bits) * LANES, LANES), LANES)


def place_kernel(bases, info, *refs):
    pieces, outs, tops, held, sems = refs[:12], refs[12:14], refs[14:16], refs[16], refs[17]
    core, feat, more = info[0], held.shape[1], tops[0].shape[0]
    copies = []
    for which, base in enumerate(bases):
        near, far, near_other, far_other = pieces[4 * which : 4 * which + 4]
        last = which == len(bases) - 1
        rows = (feat if last else bases[which + 1]) - base
        span = slice(base, base + rows)
        for position in range(BLOCKS):
            where = column_at(info, which == 1, position)
            index = position % (BLOCKS // 2)
            own, other = (near, near_other) if position < BLOCKS // 2 else (far, far_other)
            a, b = own[index], other[index]
            for kind in range(2):
                value = jnp.where(core == kind, a, b)
                held[kind, span, where] = value[:rows]
                if last:
                    tops[kind][:, where] = value[rows : rows + more]
        for kind in range(2):
            copies.append(
                pltpu.make_async_copy(
                    held.at[kind, span], outs[kind].at[pl.ds(base, rows)], sems.at[which, kind]
                )
            )
            copies[-1].start()
    for copy in copies:
        copy.wait()


def place_blocks(info, bases, feat, more, width, pieces):
    shapes = [((feat, width), BF16)] * 2 + [((more, width), BF16)] * 2
    return kernel_call(
        functools.partial(place_kernel, bases), "place", shapes, [SMEM] + [VMEM] * 12, 24, info, *pieces,
        out_specs=[ANY, ANY, VMEM, VMEM],
        scratch_shapes=[pltpu.VMEM((2, feat, width), BF16), pltpu.SemaphoreType.DMA((len(bases), 2))],
    )


def on_device(sizes, table, requests, counts, nbr_low, fan_low, nbr_top, fan_top, grad_logits,
              w1_self, w1_neigh, w2_self, w2_neigh):
    peer_count, slot_count = requests.shape
    feat, width = w1_self.shape
    middle, seeds, classes = nbr_low.shape[0], nbr_top.shape[0], grad_logits.shape[1]
    across = axis_bits("cache", sizes["cache"]) + axis_bits("tr", sizes["tr"])
    along = across[1:3] + across[:1] + across[3:]
    place = 4 * bit_of(across[0]) + 2 * bit_of(across[1]) + bit_of(across[2])
    info = jnp.stack([lax.axis_index("sub"), place]).astype(jnp.int32)
    padded = -(-classes // 32) * 32
    part = feat * 352 // 768 // 16 * 16
    last = feat - 2 * part

    asked = lax.all_to_all(requests, TRAINERS, split_axis=0, concat_axis=0, tiled=True)
    picked, done = pick_rows(asked, table)
    fetched = lax.all_to_all(
        picked.reshape(peer_count, slot_count, feat), TRAINERS, split_axis=0, concat_axis=0, tiled=True
    ).reshape(peer_count * slot_count, feat)

    adj_low, adj_top, sides, scale_top, grad_hidden, cotangent = beside(
        peer_count * slot_count, padded, counts, nbr_low.T, fan_low[None], nbr_top.T, fan_top[None],
        grad_logits.T, w2_self.T, w2_neigh.T, done,
    )
    cotangent_got = swap(cotangent, *CORE_STEP)

    low = ((middle, feat), BF16)
    mine, other = kernel_call(
        mean_kernel, "mean", [low, low], [SMEM] + [VMEM] * 3, 24, info, fetched, sides, adj_low,
    )
    got = swap(other, *CORE_STEP)
    half = ((middle, width // 2), BF16)
    hidden, grads, grads_got = [None] * 2, [None] * 2, [None] * 2
    after = mine
    for which in (1, 0):
        hidden[which], grads[which] = kernel_call(
            functools.partial(hidden_kernel, which), "hidden", [half, half], [SMEM] + [VMEM] * 5 + [ANY], 24,
            info, mine, other, w1_self, w1_neigh, grad_hidden, after,
        )
        grads_got[which] = swap(grads[which], *CORE_STEP)
        after = grads[which]
    send_half, keep_half = (grads[1], grads_got[1]), (grads[0], grads_got[0])

    blocks = (BLOCKS // 2, part, LANES)
    first_send, = kernel_call(
        functools.partial(send_across_kernel, 0), "send_across", [(blocks, BF16)],
        [SMEM] + [VMEM] * 4 + [ANY], 24, info, mine, got, *send_half, after,
    )
    first_got = swap(first_send, *across[0])
    second_send, = kernel_call(
        functools.partial(send_along_kernel, part), "send_along", [(blocks, BF16)],
        [SMEM] + [VMEM] * 6 + [ANY], 24, info, mine, got, *keep_half, *send_half, first_send,
    )
    second_got = swap(second_send, *along[0])
    first_keep, second_keep = kernel_call(
        keep_kernel, "keep", [(blocks, F32), (blocks, F32)], [SMEM] + [VMEM] * 6 + [ANY], 24,
        info, mine, got, *keep_half, *send_half, second_send,
    )
    top = ((seeds, width // 2), BF16)
    logits, *tops = kernel_call(
        top_kernel, "top", [((classes, seeds), F32), top, top, top, top], [SMEM] + [VMEM] * 6 + [ANY], 24,
        info, hidden[0], hidden[1], adj_top, scale_top, w2_self.T, w2_neigh.T, second_keep,
    )
    tops_got = [swap(tops[2], *CORE_STEP), swap(tops[3], *CORE_STEP)]
    a = Piece(across, first_got, first_keep)
    b = Piece(along, second_got, second_keep)
    after = b.first(a.first(logits))
    blocks = (BLOCKS // 2, last + padded, LANES)
    third_send, third_keep = kernel_call(
        functools.partial(last_kernel, 2 * part), "last", [(blocks, BF16), (blocks, F32)],
        [SMEM] + [VMEM] * 12 + [ANY], 24, info, mine, got, *keep_half, *send_half, cotangent, cotangent_got,
        tops[0], tops_got[0], tops[1], tops_got[1], after,
    )
    third_got = swap(third_send, *across[0])
    c = Piece(across, third_got, third_keep)
    after = third_keep
    for step in (a.second, b.second, c.first, a.meet, b.meet, c.second):
        after = step(after)
    after = a.join(after, after)
    after = c.meet(b.join(after, after))
    c.join(after, a.blocks[1])

    def both_kinds(piece):
        near, far, near_other = piece.blocks
        return near, far, near_other, swap(far, *CORE_STEP)

    pieces = both_kinds(a) + both_kinds(b) + both_kinds(c)
    w1s, w1n, w2s, w2n = place_blocks(info, (0, part, 2 * part), feat, classes, width, pieces)
    return (logits.T, w1s, w1n, w2s.T, w2n.T)


def solution(mesh):
    split, whole = P(("grp", "tr", "cache", "sub"), None), P(("grp", "tr", "cache", "sub"))
    in_specs = (split, split, whole, split, whole, split, whole, split, P(), P(), P(), P())
    out_specs = (split, P("grp", None), P("grp", None), P("grp", None), P("grp", None))
    return jax.shard_map(
        functools.partial(on_device, dict(mesh.shape)),
        mesh=mesh,
        in_specs=in_specs,
        out_specs=out_specs,
        check_vma=False,
    )
```

```python
import functools

import jax
import jax.numpy as jnp
from jax import lax
from jax.experimental import pallas as pl
from jax.experimental.pallas import tpu as pltpu
from jax.sharding import PartitionSpec as P

LANES = 128
GROUPS = ((4, 5, 6, 7), (2, 3, 1, 0))
ASK = 0
BESIDE = 3
LANDINGS = (0, 4, 5, 6, 7, 2, 3, 1)
CORE_STEP = ("sub", 2, 1)
BLOCKS = 8
TRAINERS = ("tr", "cache", "sub")
F32, BF16 = jnp.float32, jnp.bfloat16
VMEM = pl.BlockSpec(memory_space=pltpu.VMEM)
SMEM = pl.BlockSpec(memory_space=pltpu.SMEM)
ANY = pl.BlockSpec(memory_space=pl.ANY)


def params(mebibytes):
    return pltpu.CompilerParams(vmem_limit_bytes=mebibytes * 1024 * 1024)


def tdot(lhs, rhs):
    return lax.dot_general(lhs, rhs, (((0,), (0,)), ((), ())), preferred_element_type=F32)


def swap(array, axis, size, distance):
    return lax.ppermute(array, axis, [(i, i ^ distance) for i in range(size)])


def axis_bits(axis, size):
    return [(axis, size, 1 << k) for k in range(size.bit_length() - 1)]


def bit_of(step):
    axis, _, distance = step
    return lax.rem(lax.div(lax.axis_index(axis), distance), 2)


def kernel_call(body, name, outs, in_specs, mebibytes, *operands, **kwargs):
    return pl.pallas_call(
        body,
        out_shape=[jax.ShapeDtypeStruct(*out) for out in outs],
        in_specs=in_specs,
        out_specs=kwargs.pop("out_specs", [VMEM] * len(outs)),
        compiler_params=params(mebibytes),
        cost_estimate=pl.CostEstimate(flops=10**10, bytes_accessed=10**7, transcendentals=0),
        name=name,
        **kwargs,
    )(*operands)


def fold_kernel(got, keep, after, send, kept):
    half = kept.shape[0]
    send[...] = (keep[half:] + got[half:].astype(F32)).astype(BF16)
    kept[...] = keep[:half] + got[:half].astype(F32)


def add_kernel(got, keep, after, out):
    out[...] = (keep[...] + got[...].astype(F32)).astype(out.dtype)


def meet_kernel(mine, got, after, out):
    out[0] = (mine[0].astype(F32) + got[1].astype(F32)).astype(BF16)
    out[1] = (mine[1].astype(F32) + got[0].astype(F32)).astype(BF16)


def join_kernel(near, far, after, later, out):
    half = near.shape[0]
    out[:half] = near[...]
    out[half:] = far[...]


def deep_sum(keep, order):
    extra = order[3:]
    got = swap(keep[1:].astype(BF16), *order[2])
    share = keep[:1] + got.astype(F32)
    for step in extra:
        half = share.shape[1] // 2
        bit = bit_of(step)
        other = lax.dynamic_slice_in_dim(share, (1 - bit) * half, half, 1).astype(BF16)
        share = lax.dynamic_slice_in_dim(share, bit * half, half, 1)
        share = share + swap(other, *step).astype(F32)
    share = share.astype(BF16)
    for step in extra[::-1]:
        got = swap(share, *step)
        low = bit_of(step) == 0
        share = jnp.concatenate([jnp.where(low, share, got), jnp.where(low, got, share)], 1)
    return jnp.concatenate([share, swap(share, *order[2])], 0)


class Piece:
    def __init__(self, order, got, keep):
        self.order, self.got, self.keep = order, got, keep

    def first(self, after):
        count, rows, lanes = self.keep.shape
        send, self.keep = kernel_call(
            fold_kernel, "fold", [((count // 2, rows, lanes), BF16), ((count // 2, rows, lanes), F32)],
            [VMEM, VMEM, ANY], 16, self.got, self.keep, after,
        )
        self.got = swap(send, *self.order[1])
        return send

    def second(self, after):
        deep = len(self.order) > 3
        self.keep, = kernel_call(
            add_kernel, "add", [(self.keep.shape, F32 if deep else BF16)],
            [VMEM, VMEM, ANY], 16, self.got, self.keep, after,
        )
        if not deep:
            self.got = swap(self.keep, *self.order[2])
        return self.keep

    def meet(self, after):
        if len(self.order) > 3:
            self.keep = deep_sum(self.keep, self.order)
        else:
            self.keep, = kernel_call(
                meet_kernel, "meet", [(self.keep.shape, BF16)],
                [VMEM, VMEM, ANY], 16, self.keep, self.got, after,
            )
        self.got = swap(self.keep, *self.order[1])
        return self.keep

    def join(self, after, later):
        count, rows, lanes = self.keep.shape
        near, = kernel_call(
            join_kernel, "join", [((2 * count, rows, lanes), BF16)],
            [VMEM, VMEM, ANY, ANY], 16, self.keep, self.got, after, later,
        )
        far = swap(near, *self.order[0])
        self.blocks = (near, far, swap(near, *CORE_STEP))
        return near


def pair_of(info):
    return lax.rem(lax.div(info[1], 2), 2), lax.rem(info[1], 2)


def gradient(span, columns, mine, got, grad, grad_got):
    return tdot(mine[:, span], grad[:, columns]) + tdot(got[:, span], grad_got[:, columns])


def wide_pair(pair):
    return pl.ds(pl.multiple_of(pair * 2 * LANES, 2 * LANES), 2 * LANES)


def across_blocks(info, span, rows, mine, got, grad, grad_got, out):
    high, low = pair_of(info)
    for pair in range(2):
        value = gradient(span, wide_pair(jnp.bitwise_xor(pair, high)), mine, got, grad, grad_got)
        value = value.astype(out.dtype)
        out[2 * pair + low, rows] = value[:, :LANES]
        out[2 * pair + 1 - low, rows] = value[:, LANES:]


def along_blocks(info, first, span, mine, got, halves, out):
    high, low = pair_of(info)
    for bit, (grad, grad_got) in enumerate(halves):
        value = gradient(span, wide_pair(jnp.bitwise_xor(first, high)), mine, got, grad, grad_got)
        value = value.astype(out.dtype)
        out[2 * low + bit] = value[:, :LANES]
        out[2 * (1 - low) + bit] = value[:, LANES:]


def send_across_kernel(base, info, mine, got, grad, grad_got, after, out):
    rows = out.shape[1]
    across_blocks(info, slice(base, base + rows), slice(0, rows), mine, got, grad, grad_got, out)


def send_along_kernel(base, info, mine, got, grad, grad_got, far, far_got, after, out):
    span = slice(base, base + out.shape[1])
    along_blocks(info, 1, span, mine, got, ((grad, grad_got), (far, far_got)), out)


def keep_kernel(info, mine, got, grad, grad_got, far, far_got, after, out, out_along):
    rows = out.shape[1]
    across_blocks(info, slice(0, rows), slice(0, rows), mine, got, grad, grad_got, out)
    span = slice(rows, 2 * rows)
    along_blocks(info, 0, span, mine, got, ((grad, grad_got), (far, far_got)), out_along)


def last_kernel(base, info, mine, got, grad, grad_got, far, far_got, cot, cot_got, top, top_got,
                top_far, top_far_got, after, send, keep):
    rows, more = mine.shape[1] - base, cot.shape[1]
    for out, a, b, c, d in (
        (send, far, far_got, top_far, top_far_got), (keep, grad, grad_got, top, top_got)
    ):
        across_blocks(info, slice(base, base + rows), slice(0, rows), mine, got, a, b, out)
        across_blocks(info, slice(0, more), slice(rows, rows + more), cot, cot_got, c, d, out)


def pick_kernel(asked, table, out, done, onehot, held, sem):
    copy = pltpu.make_async_copy(table, held, sem)
    copy.start()
    peers, slots = asked.shape
    wide = lax.broadcasted_iota(jnp.int32, (16 * max(1, slots // 16), table.shape[0]), 1)
    columns = asked[...].T
    step = max(1, 16 // slots)
    for peer in range(0, peers, step):
        numbers = [columns[:, p : p + 1] for p in range(peer, peer + step)]
        numbers = numbers[0] if step == 1 else jnp.concatenate(numbers, 0)
        onehot[peer * slots : (peer + step) * slots] = jnp.where(numbers == wide, 1.0, 0.0).astype(BF16)
    done[...] = jnp.zeros_like(done)
    copy.wait()
    for start in range(0, out.shape[1], 256):
        span = slice(start, start + 256)
        out[:, span] = jnp.dot(onehot[...], held[:, span], preferred_element_type=F32).astype(BF16)


def pick_rows(asked, table):
    total = asked.shape[0] * asked.shape[1]
    return pl.pallas_call(
        pick_kernel,
        out_shape=[
            jax.ShapeDtypeStruct((total, table.shape[1]), BF16),
            jax.ShapeDtypeStruct((8, LANES), jnp.int32),
        ],
        in_specs=[VMEM, ANY],
        out_specs=[VMEM, VMEM],
        scratch_shapes=[
            pltpu.VMEM((total, table.shape[0]), BF16),
            pltpu.VMEM(table.shape, BF16),
            pltpu.SemaphoreType.DMA,
        ],
        compiler_params=params(56),
        name="pick_rows",
    )(asked, table)


def route_kernel(info, requests, own, other):
    for distance in range(own.shape[0]):
        at = 2 * jnp.bitwise_xor(info[2], distance)
        own[distance : distance + 1] = requests[pl.ds(at + info[0], 1)]
        other[distance : distance + 1] = requests[pl.ds(at + 1 - info[0], 1)]


def bundle_kernel(distances, own, got, after, *outs):
    for distance, out in zip(distances, outs):
        out[:1] = own[distance : distance + 1]
        out[1:] = got[distance : distance + 1]


def serve_kernel(asked, table, after, out):
    trainers, slots = asked.shape
    wide = lax.broadcasted_iota(jnp.int32, (slots, table.shape[0]), 1)
    columns = asked[...].T
    hits = [jnp.where(columns[:, t : t + 1] == wide, 1.0, 0.0).astype(BF16) for t in range(trainers)]
    out[...] = jnp.dot(jnp.concatenate(hits, 0), table[...], preferred_element_type=F32).astype(BF16)


def fetch(info, requests, table, chips, meanwhile):
    slots, feat = requests.shape[1], table.shape[1]
    ids, rows = ((chips, slots), jnp.int32), ((2 * slots, feat), BF16)
    own, other = kernel_call(route_kernel, "route", [ids, ids], [SMEM, VMEM], 16, info, requests)
    passed = swap(other, *CORE_STEP)
    after, landed = own, {}

    def bundles(distances, after):
        return dict(zip(distances, kernel_call(
            functools.partial(bundle_kernel, distances), "bundle", [((2, slots), jnp.int32)] * len(distances),
            [VMEM, VMEM, ANY], 16, own, passed, after,
        )))

    def across_chips(array, distance):
        return lax.ppermute(array, ("tr", "cache"), [(i, i ^ distance) for i in range(chips)])

    asked = bundles(GROUPS[0], own)
    for which, group in enumerate(GROUPS):
        arrived = {d: across_chips(asked[d], d) if d else asked[d] for d in group}
        for number, distance in enumerate(group):
            after, = kernel_call(
                serve_kernel, "serve", [rows], [VMEM, VMEM, ANY], 16, arrived[distance], table, after
            )
            landed[distance] = across_chips(after, distance) if distance else after
            if number == ASK and which + 1 < len(GROUPS):
                asked = bundles(GROUPS[which + 1], after)
            if distance == BESIDE:
                made = meanwhile(after)
                after = made[0]
    far = {}
    for distance in LANDINGS:
        if distance:
            landed[distance], = kernel_call(
                land_kernel, "land", [rows], [ANY, ANY], 16, landed[distance], after,
                out_specs=[ANY], input_output_aliases={0: 0},
            )
            after = landed[distance]
        far[distance] = swap(landed[distance], *CORE_STEP)
    order = range(chips)
    return [landed[d] for d in order], [far[d] for d in order], made, after


def land_kernel(rows, after, out):
    pass


def landed_kernel(chips, info, *refs):
    near, far, (sides, adjacency, after, mine, other, held) = refs[:chips], refs[chips : 2 * chips], refs[2 * chips :]
    slots = near[0].shape[0] // 2
    for distance in range(chips):
        at = 2 * jnp.bitwise_xor(info[2], distance)
        for array, first, owner in ((near, 0, at + info[0]), (far, slots, at + 1 - info[0])):
            where = pl.ds(pl.multiple_of(owner * slots, slots), slots)
            held[where] = array[distance][first : first + slots]
    mean_kernel(info, held, sides, adjacency, mine, other)


def column_of(row):
    return jnp.broadcast_to(row, (8, row.shape[1])).T[:, :1]


def count_kernel(neighbours, used, held, adjacency, live, tile):
    slots, count = neighbours.shape
    held[...] = jnp.full(held.shape, -1, jnp.int32)
    slot = lax.broadcasted_iota(jnp.int32, (slots, count), 0)
    held[:slots] = jnp.where(slot < used[...], neighbours[...], -1)
    columns = held[...].T
    wide = lax.broadcasted_iota(jnp.int32, (tile, adjacency.shape[1]), 1)
    for start in range(0, count, tile):
        total = jnp.zeros(wide.shape, F32)
        for k in range(slots):
            total = total + jnp.where(columns[start : start + tile, k : k + 1] == wide, 1.0, 0.0)
        if live is not None:
            total = total * live
        adjacency[start : start + tile] = total.astype(BF16)


def beside_kernel(counts, nbr_low, fan_low, nbr_top, fan_top, grad, w2_self, w2_neigh, done,
                  adj_low, adj_top, sides, scale_top, grad_hidden, cotangent,
                  held_low, held_top, held_grad):
    peers = counts.shape[0]
    slots = adj_low.shape[1] // peers
    lane = lax.broadcasted_iota(jnp.int32, (1, adj_low.shape[1]), 1)
    live = jnp.zeros(lane.shape, F32)
    for peer in range(peers):
        here = (lane >= peer * slots) & (lane < peer * slots + counts[peer])
        live = jnp.where(here, 1.0, live)
    count_kernel(nbr_low, fan_low, held_low, adj_low, live, 32)
    count_kernel(nbr_top, fan_top, held_top, adj_top, None, 64)
    sides[:, :1] = column_of(1.0 / (fan_low[...].astype(F32) + 1.0))
    sides[:, 1:] = column_of(live[:, : sides.shape[0]])
    scale = column_of(1.0 / (fan_top[...].astype(F32) + 1.0))
    scale_top[...] = scale
    held_grad[...] = jnp.zeros_like(held_grad)
    held_grad[: grad.shape[0]] = grad[...].astype(F32)
    cotangent[...] = held_grad[...].T.astype(BF16)
    back = (tdot(grad[...], w2_neigh[...]) * scale).astype(BF16)
    direct = tdot(grad[...], w2_self[...]) + back.astype(F32)
    seeds = back.shape[0]
    for start in range(0, grad_hidden.shape[1], 256):
        span = slice(start, start + 256)
        spread = tdot(adj_top[...], back[:, span])
        grad_hidden[:seeds, span] = (spread[:seeds] + direct[:, span]).astype(grad_hidden.dtype)
        grad_hidden[seeds:, span] = spread[seeds:].astype(grad_hidden.dtype)


def beside(inputs, padded, counts, nbr_low, fan_low, nbr_top, fan_top, grad, w2_self, w2_neigh, done):
    middle, seeds, hidden = nbr_low.shape[1], nbr_top.shape[1], w2_self.shape[1]
    shape = jax.ShapeDtypeStruct
    return pl.pallas_call(
        beside_kernel,
        out_shape=[
            shape((middle, inputs), BF16), shape((seeds, middle), BF16), shape((middle, 2), F32),
            shape((seeds, 1), F32), shape((middle, hidden), BF16), shape((seeds, padded), BF16),
        ],
        in_specs=[SMEM] + [VMEM] * 7 + [ANY],
        out_specs=[VMEM] * 6,
        scratch_shapes=[
            pltpu.VMEM((-(-nbr_low.shape[0] // 8) * 8, middle), jnp.int32),
            pltpu.VMEM((-(-nbr_top.shape[0] // 8) * 8, seeds), jnp.int32),
            pltpu.VMEM((padded, seeds), F32),
        ],
        compiler_params=params(32),
        cost_estimate=pl.CostEstimate(flops=10**10, bytes_accessed=10**7, transcendentals=0),
        name="beside",
    )(counts, nbr_low, fan_low, nbr_top, fan_top, grad, w2_self, w2_neigh, done)


def mean_kernel(info, fetched, sides, adjacency, mine, other):
    first = info[0] == 0
    middle = mine.shape[0]
    for start in range(0, mine.shape[1], 256):
        span = slice(start, start + 256)
        own = jnp.where(sides[:, 1:] > 0.0, fetched[:middle, span].astype(F32), 0.0)
        total = jnp.dot(adjacency[...], fetched[:, span], preferred_element_type=F32)
        mean = (total + own) * sides[:, :1]
        mine[:, span] = jnp.where(first, own, mean).astype(BF16)
        other[:, span] = jnp.where(first, mean, own).astype(BF16)


def hidden_kernel(which, info, mine, other, w1_self, w1_neigh, grad_hidden, after, hidden, grad_pre):
    first = info[0] == 0
    width = hidden.shape[1]
    base = jnp.bitwise_xor(lax.div(info[1], 4), which) * width
    own = jnp.where(first, mine[...], other[...])
    mean = jnp.where(first, other[...], mine[...])
    for start in range(0, width, 256):
        at = pl.ds(pl.multiple_of(base + start, 256), 256)
        span = slice(start, start + 256)
        pre_act = jnp.dot(own, w1_self[:, at], preferred_element_type=F32)
        pre_act = pre_act + jnp.dot(mean, w1_neigh[:, at], preferred_element_type=F32)
        sigma = jax.nn.sigmoid(pre_act)
        hidden[:, span] = (pre_act * sigma).astype(BF16)
        grad = grad_hidden[:, at].astype(F32) * sigma * (1.0 + pre_act * (1.0 - sigma))
        grad_pre[:, span] = grad.astype(BF16)


def top_kernel(info, near, far, adjacency, scale, w2_self, w2_neigh, after,
               logits, mine_near, mine_far, other_near, other_far):
    first = info[0] == 0
    seeds, width = mine_near.shape
    dims = (((1,), (1,)), ((), ()))
    total = jnp.zeros(logits.shape, F32)
    for which, (hidden, mine, other) in enumerate(((near, mine_near, other_near), (far, mine_far, other_far))):
        at = pl.multiple_of(jnp.bitwise_xor(lax.div(info[1], 4), which) * width, width)
        own = hidden[:seeds]
        mean = jnp.dot(adjacency[...], hidden[...], preferred_element_type=F32)
        mean = ((mean + own.astype(F32)) * scale[...]).astype(BF16)
        mine[...] = jnp.where(first, own, mean)
        other[...] = jnp.where(first, mean, own)
        columns = pl.ds(at, width)
        total = total + lax.dot_general(w2_self[:, columns], own, dims, preferred_element_type=F32)
        total = total + lax.dot_general(w2_neigh[:, columns], mean, dims, preferred_element_type=F32)
    logits[...] = total


def column_at(info, along, position):
    bits = (position % 2) * 4 + position // 2 if along else position
    return pl.ds(pl.multiple_of(jnp.bitwise_xor(info[1], bits) * LANES, LANES), LANES)


def place_kernel(bases, info, *refs):
    pieces, outs, tops, held, sems = refs[:12], refs[12:14], refs[14:16], refs[16], refs[17]
    core, feat, more = info[0], held.shape[1], tops[0].shape[0]
    copies = []
    for which, base in enumerate(bases):
        near, far, near_other, far_other = pieces[4 * which : 4 * which + 4]
        last = which == len(bases) - 1
        rows = (feat if last else bases[which + 1]) - base
        span = slice(base, base + rows)
        for position in range(BLOCKS):
            where = column_at(info, which == 1, position)
            index = position % (BLOCKS // 2)
            own, other = (near, near_other) if position < BLOCKS // 2 else (far, far_other)
            a, b = own[index], other[index]
            for kind in range(2):
                value = jnp.where(core == kind, a, b)
                held[kind, span, where] = value[:rows]
                if last:
                    tops[kind][:, where] = value[rows : rows + more]
        for kind in range(2):
            copies.append(
                pltpu.make_async_copy(
                    held.at[kind, span], outs[kind].at[pl.ds(base, rows)], sems.at[which, kind]
                )
            )
            copies[-1].start()
    for copy in copies:
        copy.wait()


def place_blocks(info, bases, feat, more, width, pieces):
    shapes = [((feat, width), BF16)] * 2 + [((more, width), BF16)] * 2
    return kernel_call(
        functools.partial(place_kernel, bases), "place", shapes, [SMEM] + [VMEM] * 12, 24, info, *pieces,
        out_specs=[ANY, ANY, VMEM, VMEM],
        scratch_shapes=[pltpu.VMEM((2, feat, width), BF16), pltpu.SemaphoreType.DMA((len(bases), 2))],
    )


def on_device(sizes, table, requests, counts, nbr_low, fan_low, nbr_top, fan_top, grad_logits,
              w1_self, w1_neigh, w2_self, w2_neigh):
    peer_count, slot_count = requests.shape
    feat, width = w1_self.shape
    middle, seeds, classes = nbr_low.shape[0], nbr_top.shape[0], grad_logits.shape[1]
    across = axis_bits("cache", sizes["cache"]) + axis_bits("tr", sizes["tr"])
    along = across[1:3] + across[:1] + across[3:]
    place = 4 * bit_of(across[0]) + 2 * bit_of(across[1]) + bit_of(across[2])
    chips = sizes["tr"] * sizes["cache"]
    chip = lax.axis_index("tr") * sizes["cache"] + lax.axis_index("cache")
    info = jnp.stack([lax.axis_index("sub"), place, chip]).astype(jnp.int32)
    padded = -(-classes // 32) * 32
    part = feat * 352 // 768 // 16 * 16
    last = feat - 2 * part

    def meanwhile(after):
        return beside(
            peer_count * slot_count, padded, counts, nbr_low.T, fan_low[None], nbr_top.T, fan_top[None],
            grad_logits.T, w2_self.T, w2_neigh.T, after,
        )

    by_chip = chips == BLOCKS and slot_count % 16 == 0
    if by_chip:
        near, far, made, after = fetch(info, requests, table, chips, meanwhile)
    else:
        asked = lax.all_to_all(requests, TRAINERS, split_axis=0, concat_axis=0, tiled=True)
        picked, done = pick_rows(asked, table)
        fetched = lax.all_to_all(
            picked.reshape(peer_count, slot_count, feat), TRAINERS, split_axis=0, concat_axis=0, tiled=True
        ).reshape(peer_count * slot_count, feat)
        made = meanwhile(done)
    adj_low, adj_top, sides, scale_top, grad_hidden, cotangent = made
    cotangent_got = swap(cotangent, *CORE_STEP)

    low = ((middle, feat), BF16)
    if by_chip:
        mine, other = kernel_call(
            functools.partial(landed_kernel, chips), "mean", [low, low], [SMEM] + [VMEM] * (2 * chips + 2) + [ANY], 24,
            info, *near, *far, sides, adj_low, after,
            scratch_shapes=[pltpu.VMEM((peer_count * slot_count, feat), BF16)],
        )
    else:
        mine, other = kernel_call(
            mean_kernel, "mean", [low, low], [SMEM] + [VMEM] * 3, 24, info, fetched, sides, adj_low,
        )
    got = swap(other, *CORE_STEP)
    half = ((middle, width // 2), BF16)
    hidden, grads, grads_got = [None] * 2, [None] * 2, [None] * 2
    after = mine
    for which in (1, 0):
        hidden[which], grads[which] = kernel_call(
            functools.partial(hidden_kernel, which), "hidden", [half, half], [SMEM] + [VMEM] * 5 + [ANY], 24,
            info, mine, other, w1_self, w1_neigh, grad_hidden, after,
        )
        grads_got[which] = swap(grads[which], *CORE_STEP)
        after = grads[which]
    send_half, keep_half = (grads[1], grads_got[1]), (grads[0], grads_got[0])

    blocks = (BLOCKS // 2, part, LANES)
    first_send, = kernel_call(
        functools.partial(send_across_kernel, 0), "send_across", [(blocks, BF16)],
        [SMEM] + [VMEM] * 4 + [ANY], 24, info, mine, got, *send_half, after,
    )
    first_got = swap(first_send, *across[0])
    second_send, = kernel_call(
        functools.partial(send_along_kernel, part), "send_along", [(blocks, BF16)],
        [SMEM] + [VMEM] * 6 + [ANY], 24, info, mine, got, *keep_half, *send_half, first_send,
    )
    second_got = swap(second_send, *along[0])
    first_keep, second_keep = kernel_call(
        keep_kernel, "keep", [(blocks, F32), (blocks, F32)], [SMEM] + [VMEM] * 6 + [ANY], 24,
        info, mine, got, *keep_half, *send_half, second_send,
    )
    top = ((seeds, width // 2), BF16)
    logits, *tops = kernel_call(
        top_kernel, "top", [((classes, seeds), F32), top, top, top, top], [SMEM] + [VMEM] * 6 + [ANY], 24,
        info, hidden[0], hidden[1], adj_top, scale_top, w2_self.T, w2_neigh.T, second_keep,
    )
    tops_got = [swap(tops[2], *CORE_STEP), swap(tops[3], *CORE_STEP)]
    a = Piece(across, first_got, first_keep)
    b = Piece(along, second_got, second_keep)
    after = b.first(a.first(logits))
    blocks = (BLOCKS // 2, last + padded, LANES)
    third_send, third_keep = kernel_call(
        functools.partial(last_kernel, 2 * part), "last", [(blocks, BF16), (blocks, F32)],
        [SMEM] + [VMEM] * 12 + [ANY], 24, info, mine, got, *keep_half, *send_half, cotangent, cotangent_got,
        tops[0], tops_got[0], tops[1], tops_got[1], after,
    )
    third_got = swap(third_send, *across[0])
    c = Piece(across, third_got, third_keep)
    after = third_keep
    for step in (a.second, b.second, c.first, a.meet, b.meet, c.second):
        after = step(after)
    after = a.join(after, after)
    after = c.meet(b.join(after, after))
    c.join(after, a.blocks[1])

    def both_kinds(piece):
        near, far, near_other = piece.blocks
        return near, far, near_other, swap(far, *CORE_STEP)

    pieces = both_kinds(a) + both_kinds(b) + both_kinds(c)
    w1s, w1n, w2s, w2n = place_blocks(info, (0, part, 2 * part), feat, classes, width, pieces)
    return (logits.T, w1s, w1n, w2s.T, w2n.T)


def solution(mesh):
    split, whole = P(("grp", "tr", "cache", "sub"), None), P(("grp", "tr", "cache", "sub"))
    in_specs = (split, split, whole, split, whole, split, whole, split, P(), P(), P(), P())
    out_specs = (split, P("grp", None), P("grp", None), P("grp", None), P("grp", None))
    return jax.shard_map(
        functools.partial(on_device, dict(mesh.shape)),
        mesh=mesh,
        in_specs=in_specs,
        out_specs=out_specs,
        check_vma=False,
    )
```

```python
import functools

import jax
import jax.numpy as jnp
from jax import lax
from jax.experimental import pallas as pl
from jax.experimental.pallas import tpu as pltpu
from jax.sharding import PartitionSpec as P

LANES = 128
GROUPS = ((5, 4, 7, 6), (3, 1, 2, 0))
ASK = 0
BESIDE = 1
LANDINGS = (0, 5, 4, 7, 3, 6, 1, 2)
CORE_STEP = ("sub", 2, 1)
BLOCKS = 8
TRAINERS = ("tr", "cache", "sub")
F32, BF16 = jnp.float32, jnp.bfloat16
VMEM = pl.BlockSpec(memory_space=pltpu.VMEM)
SMEM = pl.BlockSpec(memory_space=pltpu.SMEM)
ANY = pl.BlockSpec(memory_space=pl.ANY)


def params(mebibytes):
    return pltpu.CompilerParams(vmem_limit_bytes=mebibytes * 1024 * 1024)


def tdot(lhs, rhs):
    return lax.dot_general(lhs, rhs, (((0,), (0,)), ((), ())), preferred_element_type=F32)


def swap(array, axis, size, distance):
    return lax.ppermute(array, axis, [(i, i ^ distance) for i in range(size)])


def axis_bits(axis, size):
    return [(axis, size, 1 << k) for k in range(size.bit_length() - 1)]


def bit_of(step):
    axis, _, distance = step
    return lax.rem(lax.div(lax.axis_index(axis), distance), 2)


def kernel_call(body, name, outs, in_specs, mebibytes, *operands, **kwargs):
    return pl.pallas_call(
        body,
        out_shape=[jax.ShapeDtypeStruct(*out) for out in outs],
        in_specs=in_specs,
        out_specs=kwargs.pop("out_specs", [VMEM] * len(outs)),
        compiler_params=params(mebibytes),
        cost_estimate=pl.CostEstimate(flops=10**10, bytes_accessed=10**7, transcendentals=0),
        name=name,
        **kwargs,
    )(*operands)


def fold_kernel(got, keep, after, send, kept):
    half = kept.shape[0]
    send[...] = (keep[half:] + got[half:].astype(F32)).astype(BF16)
    kept[...] = keep[:half] + got[:half].astype(F32)


def add_kernel(got, keep, after, out):
    out[...] = (keep[...] + got[...].astype(F32)).astype(out.dtype)


def meet_kernel(mine, got, after, out):
    out[0] = (mine[0].astype(F32) + got[1].astype(F32)).astype(BF16)
    out[1] = (mine[1].astype(F32) + got[0].astype(F32)).astype(BF16)


def join_kernel(near, far, after, later, out):
    half = near.shape[0]
    out[:half] = near[...]
    out[half:] = far[...]


def deep_sum(keep, order):
    extra = order[3:]
    got = swap(keep[1:].astype(BF16), *order[2])
    share = keep[:1] + got.astype(F32)
    for step in extra:
        half = share.shape[1] // 2
        bit = bit_of(step)
        other = lax.dynamic_slice_in_dim(share, (1 - bit) * half, half, 1).astype(BF16)
        share = lax.dynamic_slice_in_dim(share, bit * half, half, 1)
        share = share + swap(other, *step).astype(F32)
    share = share.astype(BF16)
    for step in extra[::-1]:
        got = swap(share, *step)
        low = bit_of(step) == 0
        share = jnp.concatenate([jnp.where(low, share, got), jnp.where(low, got, share)], 1)
    return jnp.concatenate([share, swap(share, *order[2])], 0)


class Piece:
    def __init__(self, order, got, keep):
        self.order, self.got, self.keep = order, got, keep

    def first(self, after):
        count, rows, lanes = self.keep.shape
        send, self.keep = kernel_call(
            fold_kernel, "fold", [((count // 2, rows, lanes), BF16), ((count // 2, rows, lanes), F32)],
            [VMEM, VMEM, ANY], 16, self.got, self.keep, after,
        )
        self.got = swap(send, *self.order[1])
        return send

    def second(self, after):
        deep = len(self.order) > 3
        self.keep, = kernel_call(
            add_kernel, "add", [(self.keep.shape, F32 if deep else BF16)],
            [VMEM, VMEM, ANY], 16, self.got, self.keep, after,
        )
        if not deep:
            self.got = swap(self.keep, *self.order[2])
        return self.keep

    def meet(self, after):
        if len(self.order) > 3:
            self.keep = deep_sum(self.keep, self.order)
        else:
            self.keep, = kernel_call(
                meet_kernel, "meet", [(self.keep.shape, BF16)],
                [VMEM, VMEM, ANY], 16, self.keep, self.got, after,
            )
        self.got = swap(self.keep, *self.order[1])
        return self.keep

    def join(self, after, later):
        count, rows, lanes = self.keep.shape
        near, = kernel_call(
            join_kernel, "join", [((2 * count, rows, lanes), BF16)],
            [VMEM, VMEM, ANY, ANY], 16, self.keep, self.got, after, later,
        )
        far = swap(near, *self.order[0])
        self.blocks = (near, far, swap(near, *CORE_STEP))
        return near


def pair_of(info):
    return lax.rem(lax.div(info[1], 2), 2), lax.rem(info[1], 2)


def gradient(span, columns, mine, got, grad, grad_got):
    return tdot(mine[:, span], grad[:, columns]) + tdot(got[:, span], grad_got[:, columns])


def wide_pair(pair):
    return pl.ds(pl.multiple_of(pair * 2 * LANES, 2 * LANES), 2 * LANES)


def across_blocks(info, span, rows, mine, got, grad, grad_got, out):
    high, low = pair_of(info)
    for pair in range(2):
        value = gradient(span, wide_pair(jnp.bitwise_xor(pair, high)), mine, got, grad, grad_got)
        value = value.astype(out.dtype)
        out[2 * pair + low, rows] = value[:, :LANES]
        out[2 * pair + 1 - low, rows] = value[:, LANES:]


def along_blocks(info, first, span, mine, got, halves, out):
    high, low = pair_of(info)
    for bit, (grad, grad_got) in enumerate(halves):
        value = gradient(span, wide_pair(jnp.bitwise_xor(first, high)), mine, got, grad, grad_got)
        value = value.astype(out.dtype)
        out[2 * low + bit] = value[:, :LANES]
        out[2 * (1 - low) + bit] = value[:, LANES:]


def send_across_kernel(base, info, mine, got, grad, grad_got, after, out):
    rows = out.shape[1]
    across_blocks(info, slice(base, base + rows), slice(0, rows), mine, got, grad, grad_got, out)


def send_along_kernel(base, info, mine, got, grad, grad_got, far, far_got, after, out):
    span = slice(base, base + out.shape[1])
    along_blocks(info, 1, span, mine, got, ((grad, grad_got), (far, far_got)), out)


def keep_kernel(info, mine, got, grad, grad_got, far, far_got, after, out, out_along):
    rows = out.shape[1]
    across_blocks(info, slice(0, rows), slice(0, rows), mine, got, grad, grad_got, out)
    span = slice(rows, 2 * rows)
    along_blocks(info, 0, span, mine, got, ((grad, grad_got), (far, far_got)), out_along)


def last_kernel(base, info, mine, got, grad, grad_got, far, far_got, cot, cot_got, top, top_got,
                top_far, top_far_got, after, send, keep):
    rows, more = mine.shape[1] - base, cot.shape[1]
    for out, a, b, c, d in (
        (send, far, far_got, top_far, top_far_got), (keep, grad, grad_got, top, top_got)
    ):
        across_blocks(info, slice(base, base + rows), slice(0, rows), mine, got, a, b, out)
        across_blocks(info, slice(0, more), slice(rows, rows + more), cot, cot_got, c, d, out)


def pick_kernel(asked, table, out, done, onehot, held, sem):
    copy = pltpu.make_async_copy(table, held, sem)
    copy.start()
    peers, slots = asked.shape
    wide = lax.broadcasted_iota(jnp.int32, (16 * max(1, slots // 16), table.shape[0]), 1)
    columns = asked[...].T
    step = max(1, 16 // slots)
    for peer in range(0, peers, step):
        numbers = [columns[:, p : p + 1] for p in range(peer, peer + step)]
        numbers = numbers[0] if step == 1 else jnp.concatenate(numbers, 0)
        onehot[peer * slots : (peer + step) * slots] = jnp.where(numbers == wide, 1.0, 0.0).astype(BF16)
    done[...] = jnp.zeros_like(done)
    copy.wait()
    for start in range(0, out.shape[1], 256):
        span = slice(start, start + 256)
        out[:, span] = jnp.dot(onehot[...], held[:, span], preferred_element_type=F32).astype(BF16)


def pick_rows(asked, table):
    total = asked.shape[0] * asked.shape[1]
    return pl.pallas_call(
        pick_kernel,
        out_shape=[
            jax.ShapeDtypeStruct((total, table.shape[1]), BF16),
            jax.ShapeDtypeStruct((8, LANES), jnp.int32),
        ],
        in_specs=[VMEM, ANY],
        out_specs=[VMEM, VMEM],
        scratch_shapes=[
            pltpu.VMEM((total, table.shape[0]), BF16),
            pltpu.VMEM(table.shape, BF16),
            pltpu.SemaphoreType.DMA,
        ],
        compiler_params=params(56),
        name="pick_rows",
    )(asked, table)


def route_kernel(info, requests, own, other):
    for distance in range(own.shape[0]):
        at = 2 * jnp.bitwise_xor(info[2], distance)
        own[distance : distance + 1] = requests[pl.ds(at + info[0], 1)]
        other[distance : distance + 1] = requests[pl.ds(at + 1 - info[0], 1)]


def bundle_kernel(distances, own, got, after, *outs):
    for distance, out in zip(distances, outs):
        out[:1] = own[distance : distance + 1]
        out[1:] = got[distance : distance + 1]


def serve_kernel(asked, table, after, out):
    trainers, slots = asked.shape
    wide = lax.broadcasted_iota(jnp.int32, (slots, table.shape[0]), 1)
    columns = asked[...].T
    hits = [jnp.where(columns[:, t : t + 1] == wide, 1.0, 0.0).astype(BF16) for t in range(trainers)]
    out[...] = jnp.dot(jnp.concatenate(hits, 0), table[...], preferred_element_type=F32).astype(BF16)


def fetch(info, requests, table, chips, meanwhile):
    slots, feat = requests.shape[1], table.shape[1]
    ids, rows = ((chips, slots), jnp.int32), ((2 * slots, feat), BF16)
    own, other = kernel_call(route_kernel, "route", [ids, ids], [SMEM, VMEM], 16, info, requests)
    passed = swap(other, *CORE_STEP)
    after, landed = own, {}

    def bundles(distances, after):
        return dict(zip(distances, kernel_call(
            functools.partial(bundle_kernel, distances), "bundle", [((2, slots), jnp.int32)] * len(distances),
            [VMEM, VMEM, ANY], 16, own, passed, after,
        )))

    def across_chips(array, distance):
        return lax.ppermute(array, ("tr", "cache"), [(i, i ^ distance) for i in range(chips)])

    asked = bundles(GROUPS[0], own)
    for which, group in enumerate(GROUPS):
        arrived = {d: across_chips(asked[d], d) if d else asked[d] for d in group}
        for number, distance in enumerate(group):
            after, = kernel_call(
                serve_kernel, "serve", [rows], [VMEM, VMEM, ANY], 16, arrived[distance], table, after
            )
            landed[distance] = across_chips(after, distance) if distance else after
            if number == ASK and which + 1 < len(GROUPS):
                asked = bundles(GROUPS[which + 1], after)
            if distance == BESIDE:
                made = meanwhile(after)
                after = made[0]
    far = {}
    for distance in LANDINGS:
        if distance:
            landed[distance], = kernel_call(
                land_kernel, "land", [rows], [ANY, ANY], 16, landed[distance], after,
                out_specs=[ANY], input_output_aliases={0: 0},
            )
            after = landed[distance]
        far[distance] = swap(landed[distance], *CORE_STEP)
    order = range(chips)
    return [landed[d] for d in order], [far[d] for d in order], made, after


def land_kernel(rows, after, out):
    pass


def landed_kernel(chips, info, *refs):
    near, far, (sides, adjacency, after, mine, other, held) = refs[:chips], refs[chips : 2 * chips], refs[2 * chips :]
    slots = near[0].shape[0] // 2
    for distance in range(chips):
        at = 2 * jnp.bitwise_xor(info[2], distance)
        for array, first, owner in ((near, 0, at + info[0]), (far, slots, at + 1 - info[0])):
            where = pl.ds(pl.multiple_of(owner * slots, slots), slots)
            held[where] = array[distance][first : first + slots]
    mean_kernel(info, held, sides, adjacency, mine, other)


def column_of(row):
    return jnp.broadcast_to(row, (8, row.shape[1])).T[:, :1]


def count_kernel(neighbours, used, held, adjacency, live, tile):
    slots, count = neighbours.shape
    held[...] = jnp.full(held.shape, -1, jnp.int32)
    slot = lax.broadcasted_iota(jnp.int32, (slots, count), 0)
    held[:slots] = jnp.where(slot < used[...], neighbours[...], -1)
    columns = held[...].T
    wide = lax.broadcasted_iota(jnp.int32, (tile, adjacency.shape[1]), 1)
    for start in range(0, count, tile):
        total = jnp.zeros(wide.shape, F32)
        for k in range(slots):
            total = total + jnp.where(columns[start : start + tile, k : k + 1] == wide, 1.0, 0.0)
        if live is not None:
            total = total * live
        adjacency[start : start + tile] = total.astype(BF16)


def beside_kernel(counts, nbr_low, fan_low, nbr_top, fan_top, grad, w2_self, w2_neigh, done,
                  adj_low, adj_top, sides, scale_top, grad_hidden, cotangent,
                  held_low, held_top, held_grad):
    peers = counts.shape[0]
    slots = adj_low.shape[1] // peers
    lane = lax.broadcasted_iota(jnp.int32, (1, adj_low.shape[1]), 1)
    live = jnp.zeros(lane.shape, F32)
    for peer in range(peers):
        here = (lane >= peer * slots) & (lane < peer * slots + counts[peer])
        live = jnp.where(here, 1.0, live)
    count_kernel(nbr_low, fan_low, held_low, adj_low, live, 32)
    count_kernel(nbr_top, fan_top, held_top, adj_top, None, 64)
    sides[:, :1] = column_of(1.0 / (fan_low[...].astype(F32) + 1.0))
    sides[:, 1:] = column_of(live[:, : sides.shape[0]])
    scale = column_of(1.0 / (fan_top[...].astype(F32) + 1.0))
    scale_top[...] = scale
    held_grad[...] = jnp.zeros_like(held_grad)
    held_grad[: grad.shape[0]] = grad[...].astype(F32)
    cotangent[...] = held_grad[...].T.astype(BF16)
    back = (tdot(grad[...], w2_neigh[...]) * scale).astype(BF16)
    direct = tdot(grad[...], w2_self[...]) + back.astype(F32)
    seeds = back.shape[0]
    for start in range(0, grad_hidden.shape[1], 256):
        span = slice(start, start + 256)
        spread = tdot(adj_top[...], back[:, span])
        grad_hidden[:seeds, span] = (spread[:seeds] + direct[:, span]).astype(grad_hidden.dtype)
        grad_hidden[seeds:, span] = spread[seeds:].astype(grad_hidden.dtype)


def beside(inputs, padded, counts, nbr_low, fan_low, nbr_top, fan_top, grad, w2_self, w2_neigh, done):
    middle, seeds, hidden = nbr_low.shape[1], nbr_top.shape[1], w2_self.shape[1]
    shape = jax.ShapeDtypeStruct
    return pl.pallas_call(
        beside_kernel,
        out_shape=[
            shape((middle, inputs), BF16), shape((seeds, middle), BF16), shape((middle, 2), F32),
            shape((seeds, 1), F32), shape((middle, hidden), BF16), shape((seeds, padded), BF16),
        ],
        in_specs=[SMEM] + [VMEM] * 7 + [ANY],
        out_specs=[VMEM] * 6,
        scratch_shapes=[
            pltpu.VMEM((-(-nbr_low.shape[0] // 8) * 8, middle), jnp.int32),
            pltpu.VMEM((-(-nbr_top.shape[0] // 8) * 8, seeds), jnp.int32),
            pltpu.VMEM((padded, seeds), F32),
        ],
        compiler_params=params(32),
        cost_estimate=pl.CostEstimate(flops=10**10, bytes_accessed=10**7, transcendentals=0),
        name="beside",
    )(counts, nbr_low, fan_low, nbr_top, fan_top, grad, w2_self, w2_neigh, done)


def mean_kernel(info, fetched, sides, adjacency, mine, other):
    first = info[0] == 0
    middle = mine.shape[0]
    for start in range(0, mine.shape[1], 256):
        span = slice(start, start + 256)
        own = jnp.where(sides[:, 1:] > 0.0, fetched[:middle, span].astype(F32), 0.0)
        total = jnp.dot(adjacency[...], fetched[:, span], preferred_element_type=F32)
        mean = (total + own) * sides[:, :1]
        mine[:, span] = jnp.where(first, own, mean).astype(BF16)
        other[:, span] = jnp.where(first, mean, own).astype(BF16)


def hidden_kernel(which, info, mine, other, w1_self, w1_neigh, grad_hidden, after, hidden, grad_pre):
    first = info[0] == 0
    width = hidden.shape[1]
    base = jnp.bitwise_xor(lax.div(info[1], 4), which) * width
    own = jnp.where(first, mine[...], other[...])
    mean = jnp.where(first, other[...], mine[...])
    for start in range(0, width, 256):
        at = pl.ds(pl.multiple_of(base + start, 256), 256)
        span = slice(start, start + 256)
        pre_act = jnp.dot(own, w1_self[:, at], preferred_element_type=F32)
        pre_act = pre_act + jnp.dot(mean, w1_neigh[:, at], preferred_element_type=F32)
        sigma = jax.nn.sigmoid(pre_act)
        hidden[:, span] = (pre_act * sigma).astype(BF16)
        grad = grad_hidden[:, at].astype(F32) * sigma * (1.0 + pre_act * (1.0 - sigma))
        grad_pre[:, span] = grad.astype(BF16)


def top_kernel(info, near, far, adjacency, scale, w2_self, w2_neigh, after,
               logits, mine_near, mine_far, other_near, other_far):
    first = info[0] == 0
    seeds, width = mine_near.shape
    dims = (((1,), (1,)), ((), ()))
    total = jnp.zeros(logits.shape, F32)
    for which, (hidden, mine, other) in enumerate(((near, mine_near, other_near), (far, mine_far, other_far))):
        at = pl.multiple_of(jnp.bitwise_xor(lax.div(info[1], 4), which) * width, width)
        own = hidden[:seeds]
        mean = jnp.dot(adjacency[...], hidden[...], preferred_element_type=F32)
        mean = ((mean + own.astype(F32)) * scale[...]).astype(BF16)
        mine[...] = jnp.where(first, own, mean)
        other[...] = jnp.where(first, mean, own)
        columns = pl.ds(at, width)
        total = total + lax.dot_general(w2_self[:, columns], own, dims, preferred_element_type=F32)
        total = total + lax.dot_general(w2_neigh[:, columns], mean, dims, preferred_element_type=F32)
    logits[...] = total


def column_at(info, along, position):
    bits = (position % 2) * 4 + position // 2 if along else position
    return pl.ds(pl.multiple_of(jnp.bitwise_xor(info[1], bits) * LANES, LANES), LANES)


def place_kernel(bases, info, *refs):
    pieces, outs, tops, held, sems = refs[:12], refs[12:14], refs[14:16], refs[16], refs[17]
    core, feat, more = info[0], held.shape[1], tops[0].shape[0]
    copies = []
    for which, base in enumerate(bases):
        near, far, near_other, far_other = pieces[4 * which : 4 * which + 4]
        last = which == len(bases) - 1
        rows = (feat if last else bases[which + 1]) - base
        span = slice(base, base + rows)
        for position in range(BLOCKS):
            where = column_at(info, which == 1, position)
            index = position % (BLOCKS // 2)
            own, other = (near, near_other) if position < BLOCKS // 2 else (far, far_other)
            a, b = own[index], other[index]
            for kind in range(2):
                value = jnp.where(core == kind, a, b)
                held[kind, span, where] = value[:rows]
                if last:
                    tops[kind][:, where] = value[rows : rows + more]
        for kind in range(2):
            copies.append(
                pltpu.make_async_copy(
                    held.at[kind, span], outs[kind].at[pl.ds(base, rows)], sems.at[which, kind]
                )
            )
            copies[-1].start()
    for copy in copies:
        copy.wait()


def place_blocks(info, bases, feat, more, width, pieces):
    shapes = [((feat, width), BF16)] * 2 + [((more, width), BF16)] * 2
    return kernel_call(
        functools.partial(place_kernel, bases), "place", shapes, [SMEM] + [VMEM] * 12, 24, info, *pieces,
        out_specs=[ANY, ANY, VMEM, VMEM],
        scratch_shapes=[pltpu.VMEM((2, feat, width), BF16), pltpu.SemaphoreType.DMA((len(bases), 2))],
    )


def on_device(sizes, table, requests, counts, nbr_low, fan_low, nbr_top, fan_top, grad_logits,
              w1_self, w1_neigh, w2_self, w2_neigh):
    peer_count, slot_count = requests.shape
    feat, width = w1_self.shape
    middle, seeds, classes = nbr_low.shape[0], nbr_top.shape[0], grad_logits.shape[1]
    across = axis_bits("cache", sizes["cache"]) + axis_bits("tr", sizes["tr"])
    along = across[1:3] + across[:1] + across[3:]
    place = 4 * bit_of(across[0]) + 2 * bit_of(across[1]) + bit_of(across[2])
    chips = sizes["tr"] * sizes["cache"]
    chip = lax.axis_index("tr") * sizes["cache"] + lax.axis_index("cache")
    info = jnp.stack([lax.axis_index("sub"), place, chip]).astype(jnp.int32)
    padded = -(-classes // 32) * 32
    part = feat * 352 // 768 // 16 * 16
    last = feat - 2 * part

    def meanwhile(after):
        return beside(
            peer_count * slot_count, padded, counts, nbr_low.T, fan_low[None], nbr_top.T, fan_top[None],
            grad_logits.T, w2_self.T, w2_neigh.T, after,
        )

    by_chip = chips == BLOCKS and slot_count % 16 == 0
    if by_chip:
        near, far, made, after = fetch(info, requests, table, chips, meanwhile)
    else:
        asked = lax.all_to_all(requests, TRAINERS, split_axis=0, concat_axis=0, tiled=True)
        picked, done = pick_rows(asked, table)
        fetched = lax.all_to_all(
            picked.reshape(peer_count, slot_count, feat), TRAINERS, split_axis=0, concat_axis=0, tiled=True
        ).reshape(peer_count * slot_count, feat)
        made = meanwhile(done)
    adj_low, adj_top, sides, scale_top, grad_hidden, cotangent = made
    cotangent_got = swap(cotangent, *CORE_STEP)

    low = ((middle, feat), BF16)
    if by_chip:
        mine, other = kernel_call(
            functools.partial(landed_kernel, chips), "mean", [low, low], [SMEM] + [VMEM] * (2 * chips + 2) + [ANY], 24,
            info, *near, *far, sides, adj_low, after,
            scratch_shapes=[pltpu.VMEM((peer_count * slot_count, feat), BF16)],
        )
    else:
        mine, other = kernel_call(
            mean_kernel, "mean", [low, low], [SMEM] + [VMEM] * 3, 24, info, fetched, sides, adj_low,
        )
    got = swap(other, *CORE_STEP)
    half = ((middle, width // 2), BF16)
    hidden, grads, grads_got = [None] * 2, [None] * 2, [None] * 2
    after = mine
    for which in (1, 0):
        hidden[which], grads[which] = kernel_call(
            functools.partial(hidden_kernel, which), "hidden", [half, half], [SMEM] + [VMEM] * 5 + [ANY], 24,
            info, mine, other, w1_self, w1_neigh, grad_hidden, after,
        )
        grads_got[which] = swap(grads[which], *CORE_STEP)
        after = grads[which]
    send_half, keep_half = (grads[1], grads_got[1]), (grads[0], grads_got[0])

    blocks = (BLOCKS // 2, part, LANES)
    first_send, = kernel_call(
        functools.partial(send_across_kernel, 0), "send_across", [(blocks, BF16)],
        [SMEM] + [VMEM] * 4 + [ANY], 24, info, mine, got, *send_half, after,
    )
    first_got = swap(first_send, *across[0])
    second_send, = kernel_call(
        functools.partial(send_along_kernel, part), "send_along", [(blocks, BF16)],
        [SMEM] + [VMEM] * 6 + [ANY], 24, info, mine, got, *keep_half, *send_half, first_send,
    )
    second_got = swap(second_send, *along[0])
    first_keep, second_keep = kernel_call(
        keep_kernel, "keep", [(blocks, F32), (blocks, F32)], [SMEM] + [VMEM] * 6 + [ANY], 24,
        info, mine, got, *keep_half, *send_half, second_send,
    )
    top = ((seeds, width // 2), BF16)
    logits, *tops = kernel_call(
        top_kernel, "top", [((classes, seeds), F32), top, top, top, top], [SMEM] + [VMEM] * 6 + [ANY], 24,
        info, hidden[0], hidden[1], adj_top, scale_top, w2_self.T, w2_neigh.T, second_keep,
    )
    tops_got = [swap(tops[2], *CORE_STEP), swap(tops[3], *CORE_STEP)]
    a = Piece(across, first_got, first_keep)
    b = Piece(along, second_got, second_keep)
    after = b.first(a.first(logits))
    blocks = (BLOCKS // 2, last + padded, LANES)
    third_send, third_keep = kernel_call(
        functools.partial(last_kernel, 2 * part), "last", [(blocks, BF16), (blocks, F32)],
        [SMEM] + [VMEM] * 12 + [ANY], 24, info, mine, got, *keep_half, *send_half, cotangent, cotangent_got,
        tops[0], tops_got[0], tops[1], tops_got[1], after,
    )
    third_got = swap(third_send, *across[0])
    c = Piece(across, third_got, third_keep)
    after = third_keep
    for step in (a.second, b.second, c.first, a.meet, b.meet, c.second):
        after = step(after)
    after = a.join(after, after)
    after = c.meet(b.join(after, after))
    c.join(after, a.blocks[1])

    def both_kinds(piece):
        near, far, near_other = piece.blocks
        return near, far, near_other, swap(far, *CORE_STEP)

    pieces = both_kinds(a) + both_kinds(b) + both_kinds(c)
    w1s, w1n, w2s, w2n = place_blocks(info, (0, part, 2 * part), feat, classes, width, pieces)
    return (logits.T, w1s, w1n, w2s.T, w2n.T)


def solution(mesh):
    split, whole = P(("grp", "tr", "cache", "sub"), None), P(("grp", "tr", "cache", "sub"))
    in_specs = (split, split, whole, split, whole, split, whole, split, P(), P(), P(), P())
    out_specs = (split, P("grp", None), P("grp", None), P("grp", None), P("grp", None))
    return jax.shard_map(
        functools.partial(on_device, dict(mesh.shape)),
        mesh=mesh,
        in_specs=in_specs,
        out_specs=out_specs,
        check_vma=False,
    )
```

```python
import functools

import jax
import jax.numpy as jnp
from jax import lax
from jax.experimental import pallas as pl
from jax.experimental.pallas import tpu as pltpu
from jax.sharding import PartitionSpec as P

LANES = 128
GROUPS = ((5, 4, 7, 6), (3, 1, 2, 0))
ASK = 0
BESIDE = 1
LANDINGS = (0, 5, 4, 7, 3, 6, 1, 2)
CORE_STEP = ("sub", 2, 1)
BLOCKS = 8
TRAINERS = ("tr", "cache", "sub")
F32, BF16 = jnp.float32, jnp.bfloat16
VMEM = pl.BlockSpec(memory_space=pltpu.VMEM)
SMEM = pl.BlockSpec(memory_space=pltpu.SMEM)
ANY = pl.BlockSpec(memory_space=pl.ANY)


def params(mebibytes):
    return pltpu.CompilerParams(vmem_limit_bytes=mebibytes * 1024 * 1024)


def tdot(lhs, rhs):
    return lax.dot_general(lhs, rhs, (((0,), (0,)), ((), ())), preferred_element_type=F32)


def swap(array, axis, size, distance):
    return lax.ppermute(array, axis, [(i, i ^ distance) for i in range(size)])


def axis_bits(axis, size):
    return [(axis, size, 1 << k) for k in range(size.bit_length() - 1)]


def bit_of(step):
    axis, _, distance = step
    return lax.rem(lax.div(lax.axis_index(axis), distance), 2)


def kernel_call(body, name, outs, in_specs, mebibytes, *operands, **kwargs):
    return pl.pallas_call(
        body,
        out_shape=[jax.ShapeDtypeStruct(*out) for out in outs],
        in_specs=in_specs,
        out_specs=kwargs.pop("out_specs", [VMEM] * len(outs)),
        compiler_params=params(mebibytes),
        cost_estimate=pl.CostEstimate(flops=10**10, bytes_accessed=10**7, transcendentals=0),
        name=name,
        **kwargs,
    )(*operands)


def fold_kernel(got, keep, after, send, kept):
    half = kept.shape[0]
    send[...] = (keep[half:] + got[half:].astype(F32)).astype(BF16)
    kept[...] = keep[:half] + got[:half].astype(F32)


def add_kernel(got, keep, after, out):
    out[...] = (keep[...] + got[...].astype(F32)).astype(out.dtype)


def meet_kernel(mine, got, after, out):
    out[0] = (mine[0].astype(F32) + got[1].astype(F32)).astype(BF16)
    out[1] = (mine[1].astype(F32) + got[0].astype(F32)).astype(BF16)


def join_kernel(near, far, after, later, out):
    half = near.shape[0]
    out[:half] = near[...]
    out[half:] = far[...]


def deep_sum(keep, order):
    extra = order[3:]
    got = swap(keep[1:].astype(BF16), *order[2])
    share = keep[:1] + got.astype(F32)
    for step in extra:
        half = share.shape[1] // 2
        bit = bit_of(step)
        other = lax.dynamic_slice_in_dim(share, (1 - bit) * half, half, 1).astype(BF16)
        share = lax.dynamic_slice_in_dim(share, bit * half, half, 1)
        share = share + swap(other, *step).astype(F32)
    share = share.astype(BF16)
    for step in extra[::-1]:
        got = swap(share, *step)
        low = bit_of(step) == 0
        share = jnp.concatenate([jnp.where(low, share, got), jnp.where(low, got, share)], 1)
    return jnp.concatenate([share, swap(share, *order[2])], 0)


class Piece:
    def __init__(self, order, got, keep):
        self.order, self.got, self.keep = order, got, keep

    def first(self, after):
        count, rows, lanes = self.keep.shape
        send, self.keep = kernel_call(
            fold_kernel, "fold", [((count // 2, rows, lanes), BF16), ((count // 2, rows, lanes), F32)],
            [VMEM, VMEM, ANY], 16, self.got, self.keep, after,
        )
        self.got = swap(send, *self.order[1])
        return send

    def second(self, after):
        deep = len(self.order) > 3
        self.keep, = kernel_call(
            add_kernel, "add", [(self.keep.shape, F32 if deep else BF16)],
            [VMEM, VMEM, ANY], 16, self.got, self.keep, after,
        )
        if not deep:
            self.got = swap(self.keep, *self.order[2])
        return self.keep

    def meet(self, after):
        if len(self.order) > 3:
            self.keep = deep_sum(self.keep, self.order)
        else:
            self.keep, = kernel_call(
                meet_kernel, "meet", [(self.keep.shape, BF16)],
                [VMEM, VMEM, ANY], 16, self.keep, self.got, after,
            )
        self.got = swap(self.keep, *self.order[1])
        return self.keep

    def join(self, after, later):
        count, rows, lanes = self.keep.shape
        near, = kernel_call(
            join_kernel, "join", [((2 * count, rows, lanes), BF16)],
            [VMEM, VMEM, ANY, ANY], 16, self.keep, self.got, after, later,
        )
        far = swap(near, *self.order[0])
        self.blocks = (near, far, swap(near, *CORE_STEP))
        return near


def pair_of(info):
    return lax.rem(lax.div(info[1], 2), 2), lax.rem(info[1], 2)


def gradient(span, columns, mine, got, grad, grad_got):
    return tdot(mine[:, span], grad[:, columns]) + tdot(got[:, span], grad_got[:, columns])


def wide_pair(pair):
    return pl.ds(pl.multiple_of(pair * 2 * LANES, 2 * LANES), 2 * LANES)


def across_blocks(info, span, rows, mine, got, grad, grad_got, out):
    high, low = pair_of(info)
    for pair in range(2):
        value = gradient(span, wide_pair(jnp.bitwise_xor(pair, high)), mine, got, grad, grad_got)
        value = value.astype(out.dtype)
        out[2 * pair + low, rows] = value[:, :LANES]
        out[2 * pair + 1 - low, rows] = value[:, LANES:]


def along_blocks(info, first, span, mine, got, halves, out):
    high, low = pair_of(info)
    for bit, (grad, grad_got) in enumerate(halves):
        value = gradient(span, wide_pair(jnp.bitwise_xor(first, high)), mine, got, grad, grad_got)
        value = value.astype(out.dtype)
        out[2 * low + bit] = value[:, :LANES]
        out[2 * (1 - low) + bit] = value[:, LANES:]


def send_across_kernel(base, info, mine, got, grad, grad_got, after, out):
    rows = out.shape[1]
    across_blocks(info, slice(base, base + rows), slice(0, rows), mine, got, grad, grad_got, out)


def send_along_kernel(base, info, mine, got, grad, grad_got, far, far_got, after, out):
    span = slice(base, base + out.shape[1])
    along_blocks(info, 1, span, mine, got, ((grad, grad_got), (far, far_got)), out)


def keep_kernel(info, mine, got, grad, grad_got, far, far_got, after, out, out_along):
    rows = out.shape[1]
    across_blocks(info, slice(0, rows), slice(0, rows), mine, got, grad, grad_got, out)
    span = slice(rows, 2 * rows)
    along_blocks(info, 0, span, mine, got, ((grad, grad_got), (far, far_got)), out_along)


def last_kernel(base, info, mine, got, grad, grad_got, far, far_got, cot, cot_got, top, top_got,
                top_far, top_far_got, after, send, keep):
    rows, more = mine.shape[1] - base, cot.shape[1]
    for out, a, b, c, d in (
        (send, far, far_got, top_far, top_far_got), (keep, grad, grad_got, top, top_got)
    ):
        across_blocks(info, slice(base, base + rows), slice(0, rows), mine, got, a, b, out)
        across_blocks(info, slice(0, more), slice(rows, rows + more), cot, cot_got, c, d, out)


def pick_kernel(asked, table, out, done, onehot, held, sem):
    copy = pltpu.make_async_copy(table, held, sem)
    copy.start()
    peers, slots = asked.shape
    wide = lax.broadcasted_iota(jnp.int32, (16 * max(1, slots // 16), table.shape[0]), 1)
    columns = asked[...].T
    step = max(1, 16 // slots)
    for peer in range(0, peers, step):
        numbers = [columns[:, p : p + 1] for p in range(peer, peer + step)]
        numbers = numbers[0] if step == 1 else jnp.concatenate(numbers, 0)
        onehot[peer * slots : (peer + step) * slots] = jnp.where(numbers == wide, 1.0, 0.0).astype(BF16)
    done[...] = jnp.zeros_like(done)
    copy.wait()
    for start in range(0, out.shape[1], 256):
        span = slice(start, start + 256)
        out[:, span] = jnp.dot(onehot[...], held[:, span], preferred_element_type=F32).astype(BF16)


def pick_rows(asked, table):
    total = asked.shape[0] * asked.shape[1]
    return pl.pallas_call(
        pick_kernel,
        out_shape=[
            jax.ShapeDtypeStruct((total, table.shape[1]), BF16),
            jax.ShapeDtypeStruct((8, LANES), jnp.int32),
        ],
        in_specs=[VMEM, ANY],
        out_specs=[VMEM, VMEM],
        scratch_shapes=[
            pltpu.VMEM((total, table.shape[0]), BF16),
            pltpu.VMEM(table.shape, BF16),
            pltpu.SemaphoreType.DMA,
        ],
        compiler_params=params(56),
        name="pick_rows",
    )(asked, table)


def route_kernel(info, requests, own, other):
    for distance in range(own.shape[0]):
        at = 2 * jnp.bitwise_xor(info[2], distance)
        own[distance : distance + 1] = requests[pl.ds(at + info[0], 1)]
        other[distance : distance + 1] = requests[pl.ds(at + 1 - info[0], 1)]


def bundle_kernel(distances, own, got, after, *outs):
    for distance, out in zip(distances, outs):
        out[:1] = own[distance : distance + 1]
        out[1:] = got[distance : distance + 1]


def serve_kernel(asked, table, after, out):
    trainers, slots = asked.shape
    wide = lax.broadcasted_iota(jnp.int32, (slots, table.shape[0]), 1)
    columns = asked[...].T
    hits = [jnp.where(columns[:, t : t + 1] == wide, 1.0, 0.0).astype(BF16) for t in range(trainers)]
    out[...] = jnp.dot(jnp.concatenate(hits, 0), table[...], preferred_element_type=F32).astype(BF16)


def fetch(info, requests, table, chips, meanwhile):
    slots, feat = requests.shape[1], table.shape[1]
    ids, rows = ((chips, slots), jnp.int32), ((2 * slots, feat), BF16)
    own, other = kernel_call(route_kernel, "route", [ids, ids], [SMEM, VMEM], 16, info, requests)
    passed = swap(other, *CORE_STEP)
    after, landed = own, {}

    def bundles(distances, after):
        return dict(zip(distances, kernel_call(
            functools.partial(bundle_kernel, distances), "bundle", [((2, slots), jnp.int32)] * len(distances),
            [VMEM, VMEM, ANY], 16, own, passed, after,
        )))

    def across_chips(array, distance):
        return lax.ppermute(array, ("tr", "cache"), [(i, i ^ distance) for i in range(chips)])

    asked = bundles(GROUPS[0], own)
    for which, group in enumerate(GROUPS):
        arrived = {d: across_chips(asked[d], d) if d else asked[d] for d in group}
        for number, distance in enumerate(group):
            after, = kernel_call(
                serve_kernel, "serve", [rows], [VMEM, VMEM, ANY], 16, arrived[distance], table, after
            )
            landed[distance] = across_chips(after, distance) if distance else after
            if number == ASK and which + 1 < len(GROUPS):
                asked = bundles(GROUPS[which + 1], after)
            if distance == BESIDE:
                made = meanwhile(after)
                after = made[0]
    far = {}
    for distance in LANDINGS:
        if distance:
            landed[distance], = kernel_call(
                land_kernel, "land", [rows], [ANY, ANY], 16, landed[distance], after,
                out_specs=[ANY], input_output_aliases={0: 0},
            )
            after = landed[distance]
        far[distance] = swap(landed[distance], *CORE_STEP)
    order = range(chips)
    return [landed[d] for d in order], [far[d] for d in order], made, after


def land_kernel(rows, after, out):
    pass


def landed_kernel(chips, info, *refs):
    near, far, (sides, adjacency, after, mine, other, held) = refs[:chips], refs[chips : 2 * chips], refs[2 * chips :]
    slots = near[0].shape[0] // 2
    for distance in range(chips):
        at = 2 * jnp.bitwise_xor(info[2], distance)
        for array, first, owner in ((near, 0, at + info[0]), (far, slots, at + 1 - info[0])):
            where = pl.ds(pl.multiple_of(owner * slots, slots), slots)
            held[where] = array[distance][first : first + slots]
    mean_kernel(info, held, sides, adjacency, mine, other)


def column_of(row):
    return jnp.broadcast_to(row, (8, row.shape[1])).T[:, :1]


def count_kernel(neighbours, used, held, adjacency, live, tile):
    slots, count = neighbours.shape
    held[...] = jnp.full(held.shape, -1, jnp.int32)
    slot = lax.broadcasted_iota(jnp.int32, (slots, count), 0)
    held[:slots] = jnp.where(slot < used[...], neighbours[...], -1)
    columns = held[...].T
    wide = lax.broadcasted_iota(jnp.int32, (tile, adjacency.shape[1]), 1)
    for start in range(0, count, tile):
        total = jnp.zeros(wide.shape, F32)
        for k in range(slots):
            total = total + jnp.where(columns[start : start + tile, k : k + 1] == wide, 1.0, 0.0)
        if live is not None:
            total = total * live
        adjacency[start : start + tile] = total.astype(BF16)


def beside_kernel(counts, nbr_low, fan_low, nbr_top, fan_top, grad, w2_self, w2_neigh, done,
                  adj_low, adj_top, sides, scale_top, grad_hidden, cotangent,
                  held_low, held_top, held_grad):
    peers = counts.shape[0]
    slots = adj_low.shape[1] // peers
    lane = lax.broadcasted_iota(jnp.int32, (1, adj_low.shape[1]), 1)
    live = jnp.zeros(lane.shape, F32)
    for peer in range(peers):
        here = (lane >= peer * slots) & (lane < peer * slots + counts[peer])
        live = jnp.where(here, 1.0, live)
    count_kernel(nbr_low, fan_low, held_low, adj_low, live, 32)
    count_kernel(nbr_top, fan_top, held_top, adj_top, None, 64)
    sides[:, :1] = column_of(1.0 / (fan_low[...].astype(F32) + 1.0))
    sides[:, 1:] = column_of(live[:, : sides.shape[0]])
    scale = column_of(1.0 / (fan_top[...].astype(F32) + 1.0))
    scale_top[...] = scale
    held_grad[...] = jnp.zeros_like(held_grad)
    held_grad[: grad.shape[0]] = grad[...].astype(F32)
    cotangent[...] = held_grad[...].T.astype(BF16)
    back = (tdot(grad[...], w2_neigh[...]) * scale).astype(BF16)
    direct = tdot(grad[...], w2_self[...]) + back.astype(F32)
    seeds = back.shape[0]
    for start in range(0, grad_hidden.shape[1], 256):
        span = slice(start, start + 256)
        spread = tdot(adj_top[...], back[:, span])
        grad_hidden[:seeds, span] = (spread[:seeds] + direct[:, span]).astype(grad_hidden.dtype)
        grad_hidden[seeds:, span] = spread[seeds:].astype(grad_hidden.dtype)


def beside(inputs, padded, counts, nbr_low, fan_low, nbr_top, fan_top, grad, w2_self, w2_neigh, done):
    middle, seeds, hidden = nbr_low.shape[1], nbr_top.shape[1], w2_self.shape[1]
    shape = jax.ShapeDtypeStruct
    return pl.pallas_call(
        beside_kernel,
        out_shape=[
            shape((middle, inputs), BF16), shape((seeds, middle), BF16), shape((middle, 2), F32),
            shape((seeds, 1), F32), shape((middle, hidden), BF16), shape((seeds, padded), BF16),
        ],
        in_specs=[SMEM] + [VMEM] * 7 + [ANY],
        out_specs=[VMEM] * 6,
        scratch_shapes=[
            pltpu.VMEM((-(-nbr_low.shape[0] // 8) * 8, middle), jnp.int32),
            pltpu.VMEM((-(-nbr_top.shape[0] // 8) * 8, seeds), jnp.int32),
            pltpu.VMEM((padded, seeds), F32),
        ],
        compiler_params=params(32),
        cost_estimate=pl.CostEstimate(flops=10**10, bytes_accessed=10**7, transcendentals=0),
        name="beside",
    )(counts, nbr_low, fan_low, nbr_top, fan_top, grad, w2_self, w2_neigh, done)


def mean_kernel(info, fetched, sides, adjacency, mine, other):
    first = info[0] == 0
    middle = mine.shape[0]
    for start in range(0, mine.shape[1], 256):
        span = slice(start, start + 256)
        own = jnp.where(sides[:, 1:] > 0.0, fetched[:middle, span].astype(F32), 0.0)
        total = jnp.dot(adjacency[...], fetched[:, span], preferred_element_type=F32)
        mean = (total + own) * sides[:, :1]
        mine[:, span] = jnp.where(first, own, mean).astype(BF16)
        other[:, span] = jnp.where(first, mean, own).astype(BF16)


def hidden_kernel(which, info, mine, other, w1_self, w1_neigh, grad_hidden, after, hidden, grad_pre):
    first = info[0] == 0
    width = hidden.shape[1]
    base = jnp.bitwise_xor(lax.div(info[1], 4), which) * width
    own = jnp.where(first, mine[...], other[...])
    mean = jnp.where(first, other[...], mine[...])
    for start in range(0, width, 256):
        at = pl.ds(pl.multiple_of(base + start, 256), 256)
        span = slice(start, start + 256)
        pre_act = jnp.dot(own, w1_self[:, at], preferred_element_type=F32)
        pre_act = pre_act + jnp.dot(mean, w1_neigh[:, at], preferred_element_type=F32)
        sigma = jax.nn.sigmoid(pre_act)
        hidden[:, span] = (pre_act * sigma).astype(BF16)
        grad = grad_hidden[:, at].astype(F32) * sigma * (1.0 + pre_act * (1.0 - sigma))
        grad_pre[:, span] = grad.astype(BF16)


def top_kernel(info, near, far, adjacency, scale, w2_self, w2_neigh, after,
               logits, mine_near, mine_far, other_near, other_far):
    first = info[0] == 0
    seeds, width = mine_near.shape
    dims = (((1,), (1,)), ((), ()))
    total = jnp.zeros(logits.shape, F32)
    for which, (hidden, mine, other) in enumerate(((near, mine_near, other_near), (far, mine_far, other_far))):
        at = pl.multiple_of(jnp.bitwise_xor(lax.div(info[1], 4), which) * width, width)
        own = hidden[:seeds]
        mean = jnp.dot(adjacency[...], hidden[...], preferred_element_type=F32)
        mean = ((mean + own.astype(F32)) * scale[...]).astype(BF16)
        mine[...] = jnp.where(first, own, mean)
        other[...] = jnp.where(first, mean, own)
        columns = pl.ds(at, width)
        total = total + lax.dot_general(w2_self[:, columns], own, dims, preferred_element_type=F32)
        total = total + lax.dot_general(w2_neigh[:, columns], mean, dims, preferred_element_type=F32)
    logits[...] = total


def column_at(info, along, position):
    bits = (position % 2) * 4 + position // 2 if along else position
    return pl.ds(pl.multiple_of(jnp.bitwise_xor(info[1], bits) * LANES, LANES), LANES)


def place_kernel(bases, info, *refs):
    pieces, outs, tops, held, sems = refs[:12], refs[12:14], refs[14:16], refs[16], refs[17]
    core, feat, more = info[0], held.shape[1], tops[0].shape[0]
    copies = []
    for which, base in enumerate(bases):
        near, far, near_other, far_other = pieces[4 * which : 4 * which + 4]
        last = which == len(bases) - 1
        rows = (feat if last else bases[which + 1]) - base
        span = slice(base, base + rows)
        for position in range(BLOCKS):
            where = column_at(info, which == 1, position)
            index = position % (BLOCKS // 2)
            own, other = (near, near_other) if position < BLOCKS // 2 else (far, far_other)
            a, b = own[index], other[index]
            for kind in range(2):
                value = jnp.where(core == kind, a, b)
                held[kind, span, where] = value[:rows]
                if last:
                    tops[kind][:, where] = value[rows : rows + more]
        for kind in range(2):
            copies.append(
                pltpu.make_async_copy(
                    held.at[kind, span], outs[kind].at[pl.ds(base, rows)], sems.at[which, kind]
                )
            )
            copies[-1].start()
    for copy in copies:
        copy.wait()


def place_blocks(info, bases, feat, more, width, pieces):
    shapes = [((feat, width), BF16)] * 2 + [((more, width), BF16)] * 2
    return kernel_call(
        functools.partial(place_kernel, bases), "place", shapes, [SMEM] + [VMEM] * 12, 24, info, *pieces,
        out_specs=[ANY, ANY, VMEM, VMEM],
        scratch_shapes=[pltpu.VMEM((2, feat, width), BF16), pltpu.SemaphoreType.DMA((len(bases), 2))],
    )


def on_device(sizes, table, requests, counts, nbr_low, fan_low, nbr_top, fan_top, grad_logits,
              w1_self, w1_neigh, w2_self, w2_neigh):
    peer_count, slot_count = requests.shape
    feat, width = w1_self.shape
    middle, seeds, classes = nbr_low.shape[0], nbr_top.shape[0], grad_logits.shape[1]
    across = axis_bits("cache", sizes["cache"]) + axis_bits("tr", sizes["tr"])
    along = across[1:3] + across[:1] + across[3:]
    place = 4 * bit_of(across[0]) + 2 * bit_of(across[1]) + bit_of(across[2])
    chips = sizes["tr"] * sizes["cache"]
    chip = lax.axis_index("tr") * sizes["cache"] + lax.axis_index("cache")
    info = jnp.stack([lax.axis_index("sub"), place, chip]).astype(jnp.int32)
    padded = -(-classes // 32) * 32
    part = feat * 352 // 768 // 16 * 16
    last = feat - 2 * part

    def meanwhile(after):
        return beside(
            peer_count * slot_count, padded, counts, nbr_low.T, fan_low[None], nbr_top.T, fan_top[None],
            grad_logits.T, w2_self.T, w2_neigh.T, after,
        )

    by_chip = chips == BLOCKS and slot_count % 16 == 0
    if by_chip:
        near, far, made, after = fetch(info, requests, table, chips, meanwhile)
    else:
        asked = lax.all_to_all(requests, TRAINERS, split_axis=0, concat_axis=0, tiled=True)
        picked, done = pick_rows(asked, table)
        fetched = lax.all_to_all(
            picked.reshape(peer_count, slot_count, feat), TRAINERS, split_axis=0, concat_axis=0, tiled=True
        ).reshape(peer_count * slot_count, feat)
        made = meanwhile(done)
    adj_low, adj_top, sides, scale_top, grad_hidden, cotangent = made
    cotangent_got = swap(cotangent, *CORE_STEP)

    low = ((middle, feat), BF16)
    if by_chip:
        mine, other = kernel_call(
            functools.partial(landed_kernel, chips), "mean", [low, low], [SMEM] + [VMEM] * (2 * chips + 2) + [ANY], 24,
            info, *near, *far, sides, adj_low, after,
            scratch_shapes=[pltpu.VMEM((peer_count * slot_count, feat), BF16)],
        )
    else:
        mine, other = kernel_call(
            mean_kernel, "mean", [low, low], [SMEM] + [VMEM] * 3, 24, info, fetched, sides, adj_low,
        )
    got = swap(other, *CORE_STEP)
    half = ((middle, width // 2), BF16)
    hidden, grads, grads_got = [None] * 2, [None] * 2, [None] * 2
    after = mine
    for which in (1, 0):
        hidden[which], grads[which] = kernel_call(
            functools.partial(hidden_kernel, which), "hidden", [half, half], [SMEM] + [VMEM] * 5 + [ANY], 24,
            info, mine, other, w1_self, w1_neigh, grad_hidden, after,
        )
        grads_got[which] = swap(grads[which], *CORE_STEP)
        after = grads[which]
    send_half, keep_half = (grads[1], grads_got[1]), (grads[0], grads_got[0])

    blocks = (BLOCKS // 2, part, LANES)
    first_send, = kernel_call(
        functools.partial(send_across_kernel, 0), "send_across", [(blocks, BF16)],
        [SMEM] + [VMEM] * 4 + [ANY], 24, info, mine, got, *send_half, after,
    )
    first_got = swap(first_send, *across[0])
    second_send, = kernel_call(
        functools.partial(send_along_kernel, part), "send_along", [(blocks, BF16)],
        [SMEM] + [VMEM] * 6 + [ANY], 24, info, mine, got, *keep_half, *send_half, first_send,
    )
    second_got = swap(second_send, *along[0])
    first_keep, second_keep = kernel_call(
        keep_kernel, "keep", [(blocks, F32), (blocks, F32)], [SMEM] + [VMEM] * 6 + [ANY], 24,
        info, mine, got, *keep_half, *send_half, second_send,
    )
    top = ((seeds, width // 2), BF16)
    logits, *tops = kernel_call(
        top_kernel, "top", [((classes, seeds), F32), top, top, top, top], [SMEM] + [VMEM] * 6 + [ANY], 24,
        info, hidden[0], hidden[1], adj_top, scale_top, w2_self.T, w2_neigh.T, second_keep,
    )
    tops_got = [swap(tops[2], *CORE_STEP), swap(tops[3], *CORE_STEP)]
    a = Piece(across, first_got, first_keep)
    b = Piece(along, second_got, second_keep)
    after = b.first(a.first(logits))
    blocks = (BLOCKS // 2, last + padded, LANES)
    third_send, third_keep = kernel_call(
        functools.partial(last_kernel, 2 * part), "last", [(blocks, BF16), (blocks, F32)],
        [SMEM] + [VMEM] * 12 + [ANY], 24, info, mine, got, *keep_half, *send_half, cotangent, cotangent_got,
        tops[0], tops_got[0], tops[1], tops_got[1], after,
    )
    third_got = swap(third_send, *across[0])
    c = Piece(across, third_got, third_keep)
    after = third_keep
    after = a.second(after)
    after = c.first(after)
    after = b.second(after)
    after = c.second(after)
    after = a.meet(after)
    after = b.meet(after)
    after = a.join(after, after)
    after = c.meet(after)
    after = b.join(after, after)
    c.join(after, a.blocks[1])

    def both_kinds(piece):
        near, far, near_other = piece.blocks
        return near, far, near_other, swap(far, *CORE_STEP)

    pieces = both_kinds(a) + both_kinds(b) + both_kinds(c)
    w1s, w1n, w2s, w2n = place_blocks(info, (0, part, 2 * part), feat, classes, width, pieces)
    return (logits.T, w1s, w1n, w2s.T, w2n.T)


def solution(mesh):
    split, whole = P(("grp", "tr", "cache", "sub"), None), P(("grp", "tr", "cache", "sub"))
    in_specs = (split, split, whole, split, whole, split, whole, split, P(), P(), P(), P())
    out_specs = (split, P("grp", None), P("grp", None), P("grp", None), P("grp", None))
    return jax.shard_map(
        functools.partial(on_device, dict(mesh.shape)),
        mesh=mesh,
        in_specs=in_specs,
        out_specs=out_specs,
        check_vma=False,
    )
```
